32 devices in a mesh: dp: 4 (over z), row: 4 (over y, core), col: 2 (over x).
Axes of the slice: x: 2, y: 2, z: 4, core: 2. Of those that a mesh axis runs over, the one named last changes fastest.
Arguments:
- tokens: bfloat16 [12288, 768], P(('dp', 'row'), 'col'), may hold values from -6 to 6
- query_weight: bfloat16 [768, 768], P('col', 'row'), may hold values from -0.21875 to 0.21875
- key_weight: bfloat16 [768, 768], P('col', 'row'), may hold values from -0.21875 to 0.21875
- value_weight: bfloat16 [768, 768], P('col', 'row'), may hold values from -0.21875 to 0.21875
- query_bias: float32 [768], P('row'), may hold values from -3 to 3
- value_bias: float32 [768], P('row'), may hold values from -3 to 3
- out_weight: bfloat16 [768, 768], P('row', 'col'), may hold values from -3 to 3
- out_bias: float32 [768], P('col'), may hold values from -3 to 3
- up_weight: bfloat16 [768, 3072], P('col', 'row'), may hold values from -0.21875 to 0.21875
- up_bias: float32 [3072], P('row'), may hold values from -3 to 3
- down_weight: bfloat16 [3072, 768], P('row', 'col'), may hold values from -0.109375 to 0.109375
- down_bias: float32 [768], P('col'), may hold values from -3 to 3
- attn_gain: float32 [768], P('col'), may hold values from 0.5 to 2
- attn_shift: float32 [768], P('col'), may hold values from -3 to 3
- mlp_gain: float32 [768], P('col'), may hold values from 0.5 to 2
- mlp_shift: float32 [768], P('col'), may hold values from -3 to 3
- cotangent: bfloat16 [12288, 768], P(('dp', 'row'), 'col'), may hold values from -6 to 6
Outputs:
- outputs: bfloat16 [12288, 768], P(('dp', 'row'), 'col')
- input_grad: float32 [12288, 768], P(('dp', 'row'), 'col')
- query_weight_grad: float32 [768, 768], P(('col', 'dp'), 'row')
- key_weight_grad: float32 [768, 768], P(('col', 'dp'), 'row')
- value_weight_grad: float32 [768, 768], P(('col', 'dp'), 'row')
- query_bias_grad: float32 [768], P(('row', 'dp'))
- value_bias_grad: float32 [768], P(('row', 'dp'))
- out_weight_grad: float32 [768, 768], P('row', ('col', 'dp'))
- out_bias_grad: float32 [768], P(('col', 'dp'))
- up_weight_grad: float32 [768, 3072], P(('col', 'dp'), 'row')
- up_bias_grad: float32 [3072], P(('row', 'dp'))
- down_weight_grad: float32 [3072, 768], P('row', ('col', 'dp'))
- down_bias_grad: float32 [768], P(('col', 'dp'))
- attn_gain_grad: float32 [768], P(('col', 'dp'))
- attn_shift_grad: float32 [768], P(('col', 'dp'))
- mlp_gain_grad: float32 [768], P(('col', 'dp'))
- mlp_shift_grad: float32 [768], P(('col', 'dp'))
The draws below stay inside these ranges and needn't reach their ends.
All inputs are finite; a program needn't handle non-finite values.
Results may differ from the reference program's by a relative error of at most 0.012.
The reference program's roundings to bfloat16 on the way count: a program that leaves them out, or rounds other values in their place, can miss the bound.
Values may be sent and summed in bfloat16 or wider, within the bound.
No kernel may reach another device: no remote copies, remote signals or barrier semaphores. Data moves between devices by JAX's collectives and lax.ppermute only.
A program may use at most 128 MiB of HBM per device.

```python
import math
import jax
import jax.numpy as jnp
from jax import lax

D = 768
H = 12
HD = 64
FF = 3072
TOK_DEV = 768
QBLK = 512
SEQ = 1536
TOKENS = 12288
N_ROW = 4


def levels(key, shape, pieces, least, high):
    loudness = 1.0
    for position, shards_of in pieces:
        heights = jax.random.uniform(jax.random.fold_in(jax.random.fold_in(key, 6), position), (shards_of,), jnp.float32, least / len(pieces), high / len(pieces))
        loudness = loudness * jnp.repeat(jnp.exp(heights), shape[position] // shards_of).reshape((-1,) + (1,) * (len(shape) - 1 - position))
    return loudness


def centred(rng, dims, scale, limit, cuts=(), kind=jnp.bfloat16):
    entries = jax.random.normal(rng, dims, jnp.float32) * scale
    if len(cuts) > 0:
        entries = levels(rng, dims, cuts, -0.22, 0.18) * entries
    return jnp.clip(entries, min=-limit, max=limit).astype(kind)


def setup_inputs(seed: int = 0) -> dict:
    splits = jax.random.split(jax.random.key(seed), 18)
    tokens = centred(splits[0], (TOKENS, D), 1.0, 6.0, ((0, 16), (1, 2)))
    query_weight = centred(splits[1], (D, D), D ** -0.5, 0.21875, ((0, 2), (1, 4)))
    key_weight = centred(splits[2], (D, D), D ** -0.5, 0.21875, ((0, 2), (1, 4)))
    value_weight = centred(splits[3], (D, D), D ** -0.5, 0.21875, ((0, 2), (1, 4)))
    query_bias = centred(splits[4], (D,), 0.5, 3.0, ((0, 4),), jnp.float32)
    value_bias = centred(splits[5], (D,), 0.5, 3.0, ((0, 4),), jnp.float32)
    out_weight = centred(splits[6], (D, D), (max(D // 256, 4)) ** -0.5, 3.0, ((0, 4), (1, 2)))
    out_bias = centred(splits[7], (D,), 0.5, 3.0, ((0, 2),), jnp.float32)
    up_weight = centred(splits[8], (D, FF), D ** -0.5, 0.21875, ((0, 2), (1, 4)))
    up_bias = centred(splits[9], (FF,), 0.5, 3.0, ((0, 4),), jnp.float32)
    down_weight = centred(splits[10], (FF, D), FF ** -0.5, 0.109375, ((0, 4), (1, 2)))
    down_bias = centred(splits[11], (D,), 0.5, 3.0, ((0, 2),), jnp.float32)
    attn_gain = jnp.clip(jnp.exp(math.log(2.0) - 1.3862944 * jax.random.uniform(splits[12], (D,), jnp.float32) ** levels(splits[12], (D,), ((0, 2),), -0.2, 0.2)), 0.5, 2.0)
    attn_shift = centred(splits[13], (D,), 0.5, 3.0, ((0, 2),), jnp.float32)
    mlp_gain = jnp.clip(jnp.exp(math.log(2.0) - 1.3862944 * jax.random.uniform(splits[14], (D,), jnp.float32) ** levels(splits[14], (D,), ((0, 2),), -0.2, 0.2)), 0.5, 2.0)
    mlp_shift = centred(splits[15], (D,), 0.5, 3.0, ((0, 2),), jnp.float32)
    cotangent = centred(splits[16], (TOKENS, D), 1.0, 6.0, ((0, 16), (1, 2)))
    return dict(tokens=tokens, query_weight=query_weight, key_weight=key_weight, value_weight=value_weight, query_bias=query_bias, value_bias=value_bias, out_weight=out_weight, out_bias=out_bias, up_weight=up_weight, up_bias=up_bias, down_weight=down_weight, down_bias=down_bias, attn_gain=attn_gain, attn_shift=attn_shift, mlp_gain=mlp_gain, mlp_shift=mlp_shift, cotangent=cotangent)


@jax.custom_vjp
def low(v):
    return lax.optimization_barrier(v.astype(jnp.bfloat16)).astype(jnp.float32)

@jax.custom_vjp
def low_back(v):
    return v

def low_keep(v):
    return (low(v), None)

def low_pass(kept, grad):
    return (grad,)

def back_keep(v):
    return (v, None)

def back_low(kept, grad):
    return (low(grad),)
low.defvjp(low_keep, low_pass)
low_back.defvjp(back_keep, back_low)
epsilon = 1e-05
highest = lax.Precision.HIGHEST

def product(left, right):
    return jnp.dot(left, right, precision=highest)

def layer_norm(values, gain, shift):
    center = lax.optimization_barrier(jnp.mean(values, axis=-1, keepdims=True))
    spread = lax.optimization_barrier(jnp.mean(values * values, axis=-1, keepdims=True)) - center * center
    return (values - center) * lax.rsqrt(spread + epsilon) * gain + shift

def attend(queries, key_rows, value_rows):
    length = queries.shape[0]
    block_rows = min(QBLK, length)
    query_heads = queries.reshape(length, H, HD)
    key_heads = key_rows.reshape(length, H, HD)
    value_heads = value_rows.reshape(length, H, HD)
    score_scale = HD ** (-0.5)

    def block_out(start):
        query_block = lax.dynamic_slice_in_dim(query_heads, start, block_rows, 0)
        scores = low_back(jnp.einsum('qhd,khd->hqk', query_block, key_heads, precision=highest) * score_scale)
        row_ids = start + lax.broadcasted_iota(jnp.int32, (block_rows, length), 0)
        col_ids = lax.broadcasted_iota(jnp.int32, (block_rows, length), 1)
        scores = jnp.where((col_ids <= row_ids)[None], scores, -1e+30)
        top = lax.optimization_barrier(jnp.max(scores, axis=-1, keepdims=True))
        powers = jnp.exp(scores - top)
        probs = powers / lax.optimization_barrier(jnp.sum(powers, axis=-1, keepdims=True))
        return jnp.einsum('hqk,khd->qhd', low(probs), value_heads, precision=highest)
    starts = (jnp.arange(length // block_rows) * block_rows).astype(jnp.int32)
    blocks = lax.map(jax.checkpoint(block_out), starts)
    return blocks.reshape(length, H * HD)

def layer(inputs, query_weight, key_weight, value_weight, query_bias, value_bias, out_weight, out_bias, up_weight, up_bias, down_weight, down_bias, attn_gain, attn_shift, mlp_gain, mlp_shift):
    first = low(layer_norm(inputs, attn_gain, attn_shift))
    queries = low(low_back(product(first, query_weight) + query_bias))
    key_rows = low(low_back(product(first, key_weight)))
    value_rows = low(low_back(product(first, value_weight) + value_bias))
    attended = jax.vmap(attend)(queries.reshape(-1, SEQ, D), key_rows.reshape(-1, SEQ, D), value_rows.reshape(-1, SEQ, D))
    attended = low(low_back(attended.reshape(-1, D)))
    middle = inputs + low_back(product(attended, out_weight) + out_bias)
    second = low(layer_norm(middle, mlp_gain, mlp_shift))
    hidden_pre = low_back(product(second, up_weight) + up_bias)
    hidden = low(jax.nn.gelu(hidden_pre, approximate=True))
    return middle + low_back(product(hidden, down_weight) + down_bias)

def reference(tokens, query_weight, key_weight, value_weight, query_bias, value_bias, out_weight, out_bias, up_weight, up_bias, down_weight, down_bias, attn_gain, attn_shift, mlp_gain, mlp_shift, cotangent):
    params = tuple((item.astype(jnp.float32) for item in (query_weight, key_weight, value_weight, query_bias, value_bias, out_weight, out_bias, up_weight, up_bias, down_weight, down_bias, attn_gain, attn_shift, mlp_gain, mlp_shift)))
    group = TOK_DEV * N_ROW
    inputs = tokens.astype(jnp.float32).reshape(-1, group, D)
    upstream = cotangent.astype(jnp.float32).reshape(-1, group, D)

    def step(totals, item):
        group_in, group_cot = item
        result, pullback = jax.vjp(layer, group_in, *params)
        grads = pullback(group_cot)
        totals = tuple((total + grad for total, grad in zip(totals, grads[1:])))
        return (totals, (result.astype(jnp.bfloat16), grads[0]))
    start_totals = tuple((jnp.zeros(item.shape, jnp.float32) for item in params))
    totals, (results, input_grads) = lax.scan(step, start_totals, (inputs, upstream))
    return (results.reshape(TOKENS, D), input_grads.reshape(TOKENS, D), totals[0], totals[1], totals[2], totals[3], totals[4], totals[5], totals[6], totals[7], totals[8], totals[9], totals[10], totals[11], totals[12], totals[13], totals[14])
```

```python
import functools
import jax
import jax.numpy as jnp
from jax import lax
from jax.experimental import pallas as pl
from jax.experimental.pallas import tpu as pltpu
from jax.sharding import PartitionSpec as P

HD = 64
QB = 256
EPS = 1e-05
bf16 = jnp.bfloat16
f32 = jnp.float32


def swap_y(value):
    return lax.ppermute(value, "row", [(r, r ^ 2) for r in range(lax.axis_size("row"))])


def swap_c(value):
    return lax.ppermute(value, "row", [(r, r ^ 1) for r in range(lax.axis_size("row"))])


def swap_x(value):
    return lax.ppermute(value, "col", [(i, i ^ 1) for i in range(lax.axis_size("col"))])


def dot(left, right):
    return jnp.dot(left, right, preferred_element_type=f32)


def dot_rt(left, right):
    return lax.dot_general(left, right, (((1,), (1,)), ((), ())), preferred_element_type=f32)


def dot_lt(left, right):
    return lax.dot_general(left, right, (((0,), (0,)), ((), ())), preferred_element_type=f32)


def causal(scores):
    rows = lax.broadcasted_iota(jnp.int32, scores.shape, 0)
    cols = lax.broadcasted_iota(jnp.int32, scores.shape, 1)
    return jnp.where(cols <= rows, scores, -1e30)


def split_heads(source, target, count, scaled):
    for i in range(count):
        part = source[:, HD * i : HD * (i + 1)]
        target[i] = part * jnp.asarray(HD**-0.5, part.dtype) if i < scaled else part


def forward_kernel(heads, qkv_ref, out_ref, log_ref, qkv, outs, logs):
    head = pl.program_id(0)

    @pl.when(head == 0)
    def _():
        split_heads(qkv_ref, qkv, 3 * heads, heads)

    length = qkv_ref.shape[0]
    for low in range(0, length, QB):
        high = low + QB
        query = qkv[head, low:high, :]
        last = causal(dot_rt(query, qkv[heads + head, low:high, :]))
        top = jnp.max(last, axis=1, keepdims=True)
        if low:
            first = dot_rt(query, qkv[heads + head, 0:low, :])
            top = jnp.maximum(top, jnp.max(first, axis=1, keepdims=True))
            first = jnp.exp(first - top)
        last = jnp.exp(last - top)
        total = jnp.sum(last, axis=1, keepdims=True)
        if low:
            total = total + jnp.sum(first, axis=1, keepdims=True)
        inverse = 1.0 / total
        out = dot((last * inverse).astype(bf16), qkv[2 * heads + head, low:high, :])
        if low:
            out = out + dot((first * inverse).astype(bf16), qkv[2 * heads + head, 0:low, :])
        outs[head, low:high, :] = out.astype(bf16)
        logs[head, low:high, :] = top + jnp.log(total)

    @pl.when(head == heads - 1)
    def _():
        out_ref[...] = jnp.concatenate([outs[i] for i in range(heads)], axis=1)
        log_ref[...] = jnp.concatenate([logs[i] for i in range(heads)], axis=1)


def backward_kernel(
    heads, qkv_ref, log_ref, up_ref, grad_ref, qkv, ups, logs, grads, key_sum, value_sum
):
    head = pl.program_id(0)

    @pl.when(head == 0)
    def _():
        split_heads(qkv_ref, qkv, 3 * heads, heads)
        split_heads(up_ref, ups, heads, 0)
        for i in range(heads):
            logs[i] = log_ref[:, i : i + 1]

    length = qkv_ref.shape[0]
    key_sum[...] = jnp.zeros_like(key_sum)
    value_sum[...] = jnp.zeros_like(value_sum)
    for low in range(0, length, QB):
        high = low + QB
        query = qkv[head, low:high, :]
        up = ups[head, low:high, :]
        log = logs[head, low:high, :]
        spans = [(low, high)] + ([(0, low)] if low else [])
        parts = []
        row_dot = 0.0
        for start, stop in spans:
            scores = dot_rt(query, qkv[heads + head, start:stop, :])
            if start == low:
                scores = causal(scores)
            probs = jnp.exp(scores - log)
            prob_grad = dot_rt(up, qkv[2 * heads + head, start:stop, :])
            row_dot = row_dot + jnp.sum(prob_grad * probs, axis=1, keepdims=True)
            value_sum[:, start:stop] += dot_lt(up, probs.astype(bf16))
            parts.append((probs, prob_grad))
        query_grad = 0.0
        for (start, stop), (probs, prob_grad) in zip(spans, parts):
            score_grad = (probs * (prob_grad - row_dot)).astype(bf16)
            query_grad = query_grad + dot(score_grad, qkv[heads + head, start:stop, :])
            key_sum[:, start:stop] += dot_lt(query, score_grad)
        grads[head, low:high, :] = (query_grad * HD**-0.5).astype(bf16)
    grads[heads + head] = key_sum[...].T.astype(bf16)
    grads[2 * heads + head] = value_sum[...].T.astype(bf16)

    @pl.when(head == heads - 1)
    def _():
        grad_ref[...] = jnp.concatenate([grads[i] for i in range(3 * heads)], axis=1)


def whole(shape):
    return pl.BlockSpec(shape, lambda head: (0,) * len(shape))


def attend(qkv):
    length, width = qkv.shape
    heads = width // (3 * HD)
    pairs = heads * length * (length + QB)
    return pl.pallas_call(
        functools.partial(forward_kernel, heads),
        grid=(heads,),
        in_specs=[whole((length, width))],
        out_specs=[whole((length, heads * HD)), whole((length, heads))],
        out_shape=[
            jax.ShapeDtypeStruct((length, heads * HD), bf16),
            jax.ShapeDtypeStruct((length, heads), f32),
        ],
        scratch_shapes=[
            pltpu.VMEM((3 * heads, length, HD), bf16),
            pltpu.VMEM((heads, length, HD), bf16),
            pltpu.VMEM((heads, length, 1), f32),
        ],
        compiler_params=pltpu.CompilerParams(vmem_limit_bytes=40 * 2**20),
        cost_estimate=pl.CostEstimate(
            flops=8 * pairs * HD, bytes_accessed=length * width * 4, transcendentals=pairs
        ),
    )(qkv)


def attend_back(qkv, log, up):
    length, width = qkv.shape
    heads = width // (3 * HD)
    pairs = heads * length * (length + QB)
    return pl.pallas_call(
        functools.partial(backward_kernel, heads),
        grid=(heads,),
        in_specs=[whole((length, width)), whole((length, heads)), whole((length, heads * HD))],
        out_specs=whole((length, width)),
        out_shape=jax.ShapeDtypeStruct((length, width), bf16),
        scratch_shapes=[
            pltpu.VMEM((3 * heads, length, HD), bf16),
            pltpu.VMEM((heads, length, HD), bf16),
            pltpu.VMEM((heads, length, 1), f32),
            pltpu.VMEM((3 * heads, length, HD), bf16),
            pltpu.VMEM((HD, length), f32),
            pltpu.VMEM((HD, length), f32),
        ],
        compiler_params=pltpu.CompilerParams(vmem_limit_bytes=48 * 2**20),
        cost_estimate=pl.CostEstimate(
            flops=20 * pairs * HD, bytes_accessed=length * width * 6, transcendentals=pairs
        ),
    )(qkv, log, up)


def layer_norm(values):
    center = jnp.mean(values, axis=1, keepdims=True)
    inverse = lax.rsqrt(jnp.mean(values * values, axis=1, keepdims=True) - center * center + EPS)
    return (values - center) * inverse, inverse


def gelu_tanh(values):
    return jax.nn.gelu(values, approximate=True)


def cat(parts, axis):
    return jnp.concatenate(parts, axis=axis)


def gather_blocks(block):
    half = block.shape[0] // 2
    beside = swap_x(block)
    above = swap_y(block)
    across = cat((swap_x(above[:half]), swap_y(beside[half:])), 0)
    return block, beside, above, across


def scatter_blocks(own, beside, above, across):
    half = own.shape[0] // 2
    for_above = swap_x(across[:half].astype(bf16)).astype(f32)
    for_beside = swap_y(across[half:].astype(bf16)).astype(f32)
    beside = cat((beside[:half], beside[half:] + for_beside), 0).astype(bf16)
    above = cat((above[:half] + for_above, above[half:]), 0).astype(bf16)
    return own + swap_x(beside).astype(f32) + swap_y(above).astype(f32)


def sum_dp(value):
    return lax.psum_scatter(value.astype(bf16), "dp", scatter_dimension=0, tiled=True).astype(f32)


def place(total, value, start):
    return lax.dynamic_update_slice_in_dim(total, value, start, 0)


def local(
    tokens,
    query_weight,
    key_weight,
    value_weight,
    query_bias,
    value_bias,
    out_weight,
    out_bias,
    up_weight,
    up_bias,
    down_weight,
    down_bias,
    attn_gain,
    attn_shift,
    mlp_gain,
    mlp_shift,
    cotangent,
):
    x = lax.axis_index("col")
    row = lax.axis_index("row")
    y, c = row // 2, row % 2
    z = lax.axis_index("dp")
    n_dp = lax.axis_size("dp")
    lined = x == y
    span, half = tokens.shape
    piece = span // 2
    width = 2 * half
    length = 2 * span
    part = query_weight.shape[1]
    hid = up_weight.shape[1]

    def pick(first, second):
        return jnp.where(lined, first, second), jnp.where(lined, second, first)

    other_tokens = swap_x(tokens)
    qkv_own = cat((query_weight, key_weight, value_weight), 1)
    qkv_other = swap_y(qkv_own)
    by_feature = jnp.stack((attn_gain, attn_shift, mlp_gain, mlp_shift, out_bias, down_bias))
    by_feature = cat((by_feature, swap_x(by_feature)), 1)
    by_unit = cat((query_bias, value_bias, up_bias), 0)
    by_unit_other = swap_y(by_unit)
    qkv_keep, qkv_send = pick(qkv_own, qkv_other)
    qkv_weight = cat((qkv_keep, swap_x(qkv_send)), 0)
    unit_keep, _ = pick(by_unit, by_unit_other)
    qkv_bias = cat((unit_keep[:part], jnp.zeros((part,), f32), unit_keep[part : 2 * part]), 0)
    up_bias_all = cat((by_unit[2 * part :], by_unit_other[2 * part :]), 0)
    first_gain, first_shift, second_gain, second_shift, out_b, down_b = by_feature

    cot_keep = lax.dynamic_slice_in_dim(cotangent, x * piece, piece, 0)
    cot_send = lax.dynamic_slice_in_dim(cotangent, (1 - x) * piece, piece, 0)
    cot_own = cat((cot_keep, swap_x(cot_send)), 1)
    cot_all = cat((cot_own, swap_c(cot_own)), 0)

    up_blocks = gather_blocks(cat((out_weight, up_weight[:, : hid // 2], up_weight[:, hid // 2 :]), 0))
    down_blocks = gather_blocks(down_weight)

    inputs = cat((tokens, other_tokens), 1).astype(f32)
    first_norm, first_inv = layer_norm(inputs)
    first_in = (first_norm * first_gain + first_shift).astype(bf16)
    first_all = place(jnp.zeros((length, width), bf16), first_in, c * span)
    first_all = place(first_all, swap_c(first_in), (1 - c) * span)
    qkv = (dot(first_all, qkv_weight) + qkv_bias).astype(bf16)
    attended, logsum = attend(qkv)

    def rows_of(value, col):
        return cat(
            [
                lax.dynamic_slice_in_dim(value, cc * span + col * piece, piece, 0)
                for cc in (c, 1 - c)
            ],
            0,
        )

    att_keep = rows_of(attended, x)
    att_got = swap_x(rows_of(attended, 1 - x))
    att_all = cat(pick(att_keep, att_got), 1)
    own, beside, above, across = (block[:part] for block in up_blocks)
    out_all = cat((cat((own, beside), 1), cat((above, across), 1)), 0)
    sums = dot(att_all, out_all)
    attn_out = sums[:piece] + swap_c(sums[piece:])
    mine = lax.dynamic_slice_in_dim(inputs, x * piece, piece, 0)
    middle = mine + (attn_out + out_b)
    second_norm, second_inv = layer_norm(middle)
    second_in = (second_norm * second_gain + second_shift).astype(bf16)
    second_all = cat((second_in, swap_c(second_in)), 0)

    own, beside, above, across = (
        cat((block[part : part + half], block[part + half :]), 1) for block in up_blocks
    )
    up_all = cat((cat((own, above), 1), cat((beside, across), 1)), 0)
    own, beside, above, across = down_blocks
    down_all = cat((cat((own, beside), 1), cat((above, across), 1)), 0)
    hidden_pre = dot(second_all, up_all) + up_bias_all
    hidden, gelu_back = jax.vjp(gelu_tanh, hidden_pre)
    hidden = hidden.astype(bf16)
    hidden_grad = dot_rt(cot_all, down_all)
    pre_grad = gelu_back(hidden_grad)[0].astype(bf16)
    sums = dot_rt(pre_grad, up_all)
    second_grad = sums[:piece] + swap_c(sums[piece:])
    scaled = second_grad * second_gain
    middle_grad = cot_own.astype(f32) + second_inv * (
        scaled
        - jnp.mean(scaled, axis=1, keepdims=True)
        - second_norm * jnp.mean(scaled * second_norm, axis=1, keepdims=True)
    )
    middle_low = middle_grad.astype(bf16)
    middle_all = cat((middle_low, swap_c(middle_low)), 0)
    att_grad = dot_rt(middle_all, out_all).astype(bf16)
    grad_keep, grad_send = pick(att_grad[:, :part], att_grad[:, part:])
    grad_got = swap_x(grad_send)
    up_att = jnp.zeros((length, part), bf16)
    for value, col in ((grad_keep, x), (grad_got, 1 - x)):
        up_att = place(up_att, value[:piece], c * span + col * piece)
        up_att = place(up_att, value[piece:], (1 - c) * span + col * piece)

    sums = dot(hidden, down_all)
    mlp_out = sums[:piece] + swap_c(sums[piece:])
    result = (middle + (mlp_out + down_b)).astype(bf16)
    outputs = place(jnp.zeros((span, half), bf16), result[:, :half], x * piece)
    outputs = place(outputs, swap_x(result[:, half:]), (1 - x) * piece)

    up_g = dot_lt(second_all, pre_grad)
    down_g = dot_lt(cot_all, hidden)
    out_g = dot_lt(middle_all, att_all)

    def block(first, second):
        rows = slice(first * half, (first + 1) * half)
        return cat(
            (
                up_g[rows, second * hid : (second + 1) * hid],
                down_g[rows, second * hid : (second + 1) * hid],
                out_g[rows, second * part : (second + 1) * part],
            ),
            1,
        )

    late = sum_dp(scatter_blocks(block(0, 0), block(1, 0), block(0, 1), block(1, 1)))
    up_w_grad = late[:, :hid]
    down_w_grad = late[:, hid : 2 * hid].T
    out_w_grad = late[:, 2 * hid :].T

    mid = place(jnp.zeros((span, half), f32), middle_grad[:, :half], x * piece)
    mid = place(mid, swap_x(middle_low[:, half:]).astype(f32), (1 - x) * piece)

    qkv_grad = attend_back(qkv, logsum, up_att)
    sums = dot_rt(qkv_grad, qkv_weight)
    sums = lax.dynamic_slice_in_dim(sums, c * span, span, 0) + swap_c(
        lax.dynamic_slice_in_dim(sums, (1 - c) * span, span, 0)
    )
    first_grad = sums[:, :half] + swap_x(sums[:, half:].astype(bf16)).astype(f32)
    own_norm = first_norm[:, :half]
    scaled = first_grad * attn_gain
    means = jnp.stack((jnp.sum(scaled, axis=1), jnp.sum(scaled * own_norm, axis=1)))
    means = (means + swap_x(means)) / width
    input_grad = mid + first_inv * (
        scaled - means[0][:, None] - own_norm * means[1][:, None]
    )

    qkv_g = dot_lt(first_all, qkv_grad)
    qkv_g_got = swap_x(qkv_g[half:].astype(bf16)).astype(f32)
    g_keep, g_send = pick(qkv_g[:half], qkv_g_got)
    qkv_w_grad = sum_dp(g_keep + swap_y(g_send.astype(bf16)).astype(f32))

    def at(vector, start, total):
        return lax.dynamic_update_slice(jnp.zeros((total,), f32), vector, (start,))

    def features(vector):
        return at(vector[:half], x * half, width) + at(vector[half:], (1 - x) * half, width)

    pre_sum = jnp.sum(pre_grad.astype(f32), axis=0)
    n_row = 2 * 2
    early = cat(
        (
            at(pre_sum[:hid], row * hid, n_row * hid)
            + at(pre_sum[hid:], (2 * (1 - y) + c) * hid, n_row * hid),
            features(jnp.sum(middle_low.astype(f32), axis=0)),
            at(jnp.sum(cotangent.astype(f32), axis=0), x * half, width),
            features(jnp.sum(second_grad * second_norm, axis=0)),
            features(jnp.sum(second_grad, axis=0)),
        ),
        0,
    )
    early = lax.psum(early, ("dp", "row", "col"))
    bias_sum = jnp.sum(qkv_grad.astype(f32), axis=0)
    group = (2 * x + c) * part
    final = cat(
        (
            at(bias_sum[:part], group, n_row * part),
            at(bias_sum[2 * part :], group, n_row * part),
            at(jnp.sum(first_grad * own_norm, axis=0), x * half, width),
            at(jnp.sum(first_grad, axis=0), x * half, width),
        ),
        0,
    )
    final = lax.psum(final, ("dp", "row", "col"))

    def take(vector, base, index, size):
        chunk = size // n_dp
        return lax.dynamic_slice(vector, (base + index * size + z * chunk,), (chunk,))

    base = n_row * hid
    return (
        outputs,
        input_grad,
        qkv_w_grad[:, :part],
        qkv_w_grad[:, part : 2 * part],
        qkv_w_grad[:, 2 * part :],
        take(final, 0, row, part),
        take(final, n_row * part, row, part),
        out_w_grad,
        take(early, base, x, half),
        up_w_grad,
        take(early, 0, row, hid),
        down_w_grad,
        take(early, base + width, x, half),
        take(final, 2 * n_row * part, x, half),
        take(final, 2 * n_row * part + width, x, half),
        take(early, base + 2 * width, x, half),
        take(early, base + 3 * width, x, half),
    )


def solution(mesh):
    placed = (
        P(("dp", "row"), "col"),
        P("col", "row"),
        P("col", "row"),
        P("col", "row"),
        P("row"),
        P("row"),
        P("row", "col"),
        P("col"),
        P("col", "row"),
        P("row"),
        P("row", "col"),
        P("col"),
        P("col"),
        P("col"),
        P("col"),
        P("col"),
        P(("dp", "row"), "col"),
    )
    return jax.shard_map(
        local,
        mesh=mesh,
        in_specs=placed,
        out_specs=(
            P(("dp", "row"), "col"),
            P(("dp", "row"), "col"),
            P(("col", "dp"), "row"),
            P(("col", "dp"), "row"),
            P(("col", "dp"), "row"),
            P(("row", "dp")),
            P(("row", "dp")),
            P("row", ("col", "dp")),
            P(("col", "dp")),
            P(("col", "dp"), "row"),
            P(("row", "dp")),
            P("row", ("col", "dp")),
            P(("col", "dp")),
            P(("col", "dp")),
            P(("col", "dp")),
            P(("col", "dp")),
            P(("col", "dp")),
        ),
        check_vma=False,
    )
```

```python
import functools
import jax
import jax.numpy as jnp
from jax import lax
from jax.experimental import pallas as pl
from jax.experimental.pallas import tpu as pltpu
from jax.sharding import PartitionSpec as P

HD = 64
QB = 256
EPS = 1e-05
bf16 = jnp.bfloat16
f32 = jnp.float32


def swap_y(value):
    return lax.ppermute(value, "row", [(r, r ^ 2) for r in range(lax.axis_size("row"))])


def swap_c(value):
    return lax.ppermute(value, "row", [(r, r ^ 1) for r in range(lax.axis_size("row"))])


def swap_x(value):
    return lax.ppermute(value, "col", [(i, i ^ 1) for i in range(lax.axis_size("col"))])


def swap_z(value):
    return lax.ppermute(value, "dp", [(i, i ^ 1) for i in range(lax.axis_size("dp"))])


def dot(left, right):
    return jnp.dot(left, right, preferred_element_type=f32)


def dot_rt(left, right):
    return lax.dot_general(left, right, (((1,), (1,)), ((), ())), preferred_element_type=f32)


def dot_lt(left, right):
    return lax.dot_general(left, right, (((0,), (0,)), ((), ())), preferred_element_type=f32)


def causal(scores):
    rows = lax.broadcasted_iota(jnp.int32, scores.shape, 0)
    cols = lax.broadcasted_iota(jnp.int32, scores.shape, 1)
    return jnp.where(cols <= rows, scores, -1e30)


def split_heads(source, target, count, scaled):
    for i in range(count):
        part = source[:, HD * i : HD * (i + 1)]
        target[i] = part * jnp.asarray(HD**-0.5, part.dtype) if i < scaled else part


def forward_kernel(heads, place_ref, in_ref, keep_ref, got_ref, bias_ref, qkv_ref, own_ref, send_ref, log_ref, weight, qkv, outs, logs):
    head = pl.program_id(0)
    length = qkv_ref.shape[0]
    half = keep_ref.shape[0]

    @pl.when(head == 0)
    def _():
        weight[:half] = keep_ref[...]
        weight[half:] = got_ref[...]
        qkv_ref[...] = (dot(in_ref[...], weight[...]) + bias_ref[...]).astype(bf16)
        split_heads(qkv_ref, qkv, 3 * heads, heads)

    for low in range(0, length, QB):
        high = low + QB
        query = qkv[head, low:high, :]
        last = causal(dot_rt(query, qkv[heads + head, low:high, :]))
        top = jnp.max(last, axis=1, keepdims=True)
        if low:
            first = dot_rt(query, qkv[heads + head, 0:low, :])
            top = jnp.maximum(top, jnp.max(first, axis=1, keepdims=True))
            first = jnp.exp(first - top)
        last = jnp.exp(last - top)
        total = jnp.sum(last, axis=1, keepdims=True)
        if low:
            total = total + jnp.sum(first, axis=1, keepdims=True)
        inverse = 1.0 / total
        out = dot((last * inverse).astype(bf16), qkv[2 * heads + head, low:high, :])
        if low:
            out = out + dot((first * inverse).astype(bf16), qkv[2 * heads + head, 0:low, :])
        outs[head, low:high, :] = out.astype(bf16)
        logs[head, low:high, :] = top + jnp.log(total)

    @pl.when(head == heads - 1)
    def _():
        piece = length // 4
        x, c = place_ref[0], place_ref[2]
        for target, col in ((own_ref, x), (send_ref, 1 - x)):
            for i, core in enumerate((c, 1 - c)):
                start = pl.multiple_of((2 * core + col) * piece, piece)
                target[i * piece : (i + 1) * piece, :] = jnp.concatenate(
                    [outs[j, pl.ds(start, piece), :] for j in range(heads)], axis=1
                )
        log_ref[...] = jnp.concatenate([logs[i] for i in range(heads)], axis=1)


def backward_kernel(
    heads, place_ref, qkv_ref, log_ref, keep_ref, got_ref, turned_ref,
    grad_ref, own_ref, send_ref, bias_ref,
    qkv, ups, logs, grads, key_sum, value_sum,
):
    head = pl.program_id(0)
    length = qkv_ref.shape[0]

    @pl.when(head == 0)
    def _():
        split_heads(qkv_ref, qkv, 3 * heads, heads)
        piece = length // 4
        x, c = place_ref[0], place_ref[2]
        for source, col in ((keep_ref, x), (got_ref, 1 - x)):
            for i, core in enumerate((c, 1 - c)):
                start = pl.multiple_of((2 * core + col) * piece, piece)
                for j in range(heads):
                    ups[j, pl.ds(start, piece), :] = source[
                        i * piece : (i + 1) * piece, j * HD : (j + 1) * HD
                    ]
        for i in range(heads):
            logs[i] = log_ref[:, i : i + 1]

    key_sum[...] = jnp.zeros_like(key_sum)
    value_sum[...] = jnp.zeros_like(value_sum)
    for low in range(0, length, QB):
        high = low + QB
        query = qkv[head, low:high, :]
        up = ups[head, low:high, :]
        log = logs[head, low:high, :]
        spans = [(low, high)] + ([(0, low)] if low else [])
        parts = []
        row_dot = 0.0
        for start, stop in spans:
            scores = dot_rt(query, qkv[heads + head, start:stop, :])
            if start == low:
                scores = causal(scores)
            probs = jnp.exp(scores - log)
            prob_grad = dot_rt(up, qkv[2 * heads + head, start:stop, :])
            row_dot = row_dot + jnp.sum(prob_grad * probs, axis=1, keepdims=True)
            value_sum[:, start:stop] += dot_lt(up, probs.astype(bf16))
            parts.append((probs, prob_grad))
        query_grad = 0.0
        for (start, stop), (probs, prob_grad) in zip(spans, parts):
            score_grad = (probs * (prob_grad - row_dot)).astype(bf16)
            query_grad = query_grad + dot(score_grad, qkv[heads + head, start:stop, :])
            key_sum[:, start:stop] += dot_lt(query, score_grad)
        grads[head, low:high, :] = (query_grad * HD**-0.5).astype(bf16)
    grads[heads + head] = key_sum[...].T.astype(bf16)
    grads[2 * heads + head] = value_sum[...].T.astype(bf16)

    @pl.when(head == heads - 1)
    def _():
        half = own_ref.shape[0]
        grad_ref[...] = jnp.concatenate([grads[i] for i in range(3 * heads)], axis=1)
        total = dot(turned_ref[...], grad_ref[...])
        own_ref[...] = total[:half]
        send_ref[...] = total[half:].astype(bf16)
        bias_ref[...] = jnp.sum(grad_ref[...].astype(f32), axis=0, keepdims=True)


def whole(shape):
    return pl.BlockSpec(shape, lambda head: (0,) * len(shape))


COST = pl.CostEstimate(flops=1, bytes_accessed=1, transcendentals=0)
LONG = pl.CostEstimate(flops=4 * 10**10, bytes_accessed=1, transcendentals=0)
SCALARS = pl.BlockSpec(memory_space=pltpu.SMEM)


def struct(dtype, *shape):
    return jax.ShapeDtypeStruct(shape, dtype)


def attend(place, first_all, keep, got, bias):
    length = first_all.shape[0]
    width = keep.shape[1]
    heads = width // (3 * HD)
    shapes = [
        struct(bf16, length, width),
        struct(bf16, length // 2, heads * HD),
        struct(bf16, length // 2, heads * HD),
        struct(f32, length, heads),
    ]
    return pl.pallas_call(
        functools.partial(forward_kernel, heads),
        name="attend",
        grid=(heads,),
        in_specs=[SCALARS] + [whole(v.shape) for v in (first_all, keep, got, bias)],
        out_specs=[whole(v.shape) for v in shapes],
        out_shape=shapes,
        scratch_shapes=[
            pltpu.VMEM((first_all.shape[1], width), bf16),
            pltpu.VMEM((3 * heads, length, HD), bf16),
            pltpu.VMEM((heads, length, HD), bf16),
            pltpu.VMEM((heads, length, 1), f32),
        ],
        compiler_params=pltpu.CompilerParams(vmem_limit_bytes=48 * 2**20),
        cost_estimate=LONG,
    )(place, first_all, keep, got, bias)


def attend_back(place, qkv, log, keep, got, turned):
    length, width = qkv.shape
    heads = width // (3 * HD)
    half = turned.shape[0] // 2
    shapes = [
        struct(bf16, length, width),
        struct(f32, half, width),
        struct(bf16, half, width),
        struct(f32, 1, width),
    ]
    return pl.pallas_call(
        functools.partial(backward_kernel, heads),
        name="attend_back",
        grid=(heads,),
        in_specs=[SCALARS] + [whole(v.shape) for v in (qkv, log, keep, got, turned)],
        out_specs=[whole(v.shape) for v in shapes],
        out_shape=shapes,
        scratch_shapes=[
            pltpu.VMEM((3 * heads, length, HD), bf16),
            pltpu.VMEM((heads, length, HD), bf16),
            pltpu.VMEM((heads, length, 1), f32),
            pltpu.VMEM((3 * heads, length, HD), bf16),
            pltpu.VMEM((HD, length), f32),
            pltpu.VMEM((HD, length), f32),
        ],
        compiler_params=pltpu.CompilerParams(vmem_limit_bytes=52 * 2**20),
        cost_estimate=LONG,
    )(place, qkv, log, keep, got, turned)


def layer_norm(values):
    center = jnp.mean(values, axis=1, keepdims=True)
    inverse = lax.rsqrt(jnp.mean(values * values, axis=1, keepdims=True) - center * center + EPS)
    return (values - center) * inverse, inverse


def norm_back(upstream, normed, inverse, gain):
    scaled = upstream * gain
    return inverse * (
        scaled
        - jnp.mean(scaled, axis=1, keepdims=True)
        - normed * jnp.mean(scaled * normed, axis=1, keepdims=True)
    )


def cat(parts, axis):
    return jnp.concatenate(parts, axis=axis)


VECTOR = pl.BlockSpec(memory_space=pltpu.VMEM)
ANYWHERE = pl.BlockSpec(memory_space=pl.ANY)


def call(kernel, name, place, inputs, shapes, scratch=(), spaces=None, cost=COST):
    ins, outs = spaces or ([VECTOR] * len(inputs), [VECTOR] * len(shapes))
    return pl.pallas_call(
        kernel,
        name=name,
        in_specs=[SCALARS] + list(ins),
        out_specs=list(outs),
        out_shape=list(shapes),
        scratch_shapes=list(scratch),
        compiler_params=pltpu.CompilerParams(vmem_limit_bytes=48 * 2**20),
        cost_estimate=cost,
    )(place, *inputs)


def first_norm_kernel(
    place_ref, own_ref, other_ref, core_own_ref, core_other_ref, params_ref,
    all_ref, turned_ref, chip_ref,
):
    x, c = place_ref[0], place_ref[2]
    span = own_ref.shape[0]
    piece = span // 2
    for i, (left, right) in enumerate(((own_ref, other_ref), (core_own_ref, core_other_ref))):
        start = pl.multiple_of((c if i == 0 else 1 - c) * span, span)
        values = cat((left[...], right[...]), 1).astype(f32)
        normed, _ = layer_norm(values)
        rounded = (normed * params_ref[0:1] + params_ref[1:2]).astype(bf16)
        all_ref[pl.ds(start, span), :] = rounded
        turned_ref[:, pl.ds(start, span)] = rounded.T
        rows = pl.ds(pl.multiple_of(x * piece, piece), piece)
        chip_ref[i * piece : (i + 1) * piece, :] = cat((left[rows, :], right[rows, :]), 1)


def upstream_kernel(place_ref, own_ref, other_ref, core_own_ref, core_other_ref, all_ref, turned_ref):
    piece = own_ref.shape[0]
    for i, (left, right) in enumerate(((own_ref, other_ref), (core_own_ref, core_other_ref))):
        values = cat((left[...], right[...]), 1)
        all_ref[i * piece : (i + 1) * piece, :] = values
        turned_ref[:, i * piece : (i + 1) * piece] = values.T


def pack_qkv_kernel(place_ref, query_hbm, key_hbm, value_hbm, all_ref, parts, sems):
    copies = [
        pltpu.make_async_copy(source, parts.at[i], sems.at[i])
        for i, source in enumerate((query_hbm, key_hbm, value_hbm))
    ]
    for copy in copies:
        copy.start()
    for copy in copies:
        copy.wait()
    all_ref[...] = cat((parts[0], parts[1], parts[2]), 1)


def pack_kernel(
    place_ref, up_ref, down_ref, cot_ref, first, second, keep_ref, send_ref, sum_ref
):
    x, lead = place_ref[0], place_ref[3]
    half = first.shape[1]
    piece = keep_ref.shape[0]
    for i, target in ((lead, first), (1 - lead, second)):
        units = pl.ds(pl.multiple_of(i * half, half), half)
        target[:half] = up_ref[:, units]
        target[half:] = down_ref[units]
    for target, col in ((keep_ref, x), (send_ref, 1 - x)):
        target[...] = cot_ref[pl.ds(pl.multiple_of(col * piece, piece), piece), :]
    sum_ref[...] = jnp.sum(cot_ref[...].astype(f32), axis=0, keepdims=True)


def out_kernel(place_ref, keep_ref, got_ref, weight_ref, sum_ref, *send_refs):
    lined = place_ref[0] == place_ref[1]
    keep, got = keep_ref[...], got_ref[...]
    values = cat((jnp.where(lined, keep, got), jnp.where(lined, got, keep)), 1)
    total = dot(values, weight_ref[...])
    sum_ref[...] = total
    rows = send_refs[0].shape[0]
    for i, send_ref in enumerate(send_refs):
        send_ref[...] = total[i * rows : (i + 1) * rows].astype(bf16)


def unit_tiles(count):
    step = 512
    return [(low, min(low + step, count)) for low in range(0, count, step)]


def unit_kernel(
    place_ref, params_ref, bias_ref, sum_hbm, got0, got1, got2, got3, chip_hbm, upstream_hbm, turned_hbm,
    own0, own1, beside0, beside1, above0, above1, across0, across1,
    middle_hbm, back_hbm, back0, back1, back2, back3,
    own0_g, own1_g, beside0_g, beside1_g, above0_g, above1_g, across0_g, across1_g,
    result_hbm, result_send_hbm, bias_sum_ref,
    sums, got, chip, upstream, turned, up, down, second, second_turned, hidden, grads,
    middle, back, back_send, own_g, pair_g, across_g, result, result_send, in_sems, out_sems,
):
    lead = place_ref[3]
    half = own0.shape[1]
    rows = got0.shape[0]
    piece = half
    started, pending = [], []

    def fetch(source, target):
        copy = pltpu.make_async_copy(source, target, in_sems.at[len(started)])
        copy.start()
        started.append(copy)
        return copy

    def put(source, target):
        copy = pltpu.make_async_copy(source, target, out_sems.at[len(pending)])
        copy.start()
        pending.append(copy)

    first = [fetch(sum_hbm, sums), fetch(chip_hbm, chip)]
    for i, source in enumerate((got0, got1, got2, got3)):
        first.append(fetch(source, got.at[pl.ds(((i + 2) % 4) * rows, rows)]))
    ups, downs = [], []
    for base, left, right in ((0, (own0, own1), (beside0, beside1)), (2, (above0, above1), (across0, across1))):
        for i in range(2):
            number = base + (lead if i == 0 else 1 - lead)
            units = pl.ds(pl.multiple_of(number * half, half), half)
            for j, source in enumerate((left[i], right[i])):
                features = pl.ds(j * half, half)
                ups.append(fetch(source.at[pl.ds(0, half)], up.at[features, units]))
                downs.append(fetch(source.at[pl.ds(half, half)], down.at[units, features]))
    downs.append(fetch(upstream_hbm, upstream))
    later = fetch(turned_hbm, turned)

    for copy in first:
        copy.wait()
    middle[...] = chip[...].astype(f32) + (sums[...] + got[...].astype(f32) + params_ref[4:5])
    put(middle, middle_hbm)
    normed, _ = layer_norm(middle[...])
    second[...] = (normed * params_ref[2:3] + params_ref[3:4]).astype(bf16)
    for copy in ups + downs:
        copy.wait()
    root = 0.7978845608028654
    total = None
    for low, high in unit_tiles(up.shape[1]):
        pre = dot(second[...], up[:, low:high]) + bias_ref[:, low:high]
        square = pre * pre
        curve = jnp.tanh(root * (pre + 0.044715 * (square * pre)))
        share = 0.5 * (1.0 + curve)
        hidden[:, low:high] = (pre * share).astype(bf16)
        slope = share + (0.5 * root) * pre * (1.0 - curve * curve) * (1.0 + 0.134145 * square)
        grad = (dot_rt(upstream[...], down[low:high, :]) * slope).astype(bf16)
        grads[:, low:high] = grad
        bias_sum_ref[:, low:high] = jnp.sum(grad.astype(f32), axis=0, keepdims=True)
        part = dot_rt(grad, up[:, low:high])
        total = part if total is None else total + part
    back[...] = total
    back_send[...] = total.astype(bf16)
    put(back, back_hbm)
    for i, target in enumerate((back0, back1, back2, back3)):
        put(back_send.at[pl.ds(i * rows, rows)], target)

    second_turned[...] = second[...].T
    later.wait()
    targets = (
        (own_g.at[0], own0_g, pair_g.at[0], beside0_g),
        (own_g.at[1], own1_g, pair_g.at[1], beside1_g),
        (pair_g.at[2], above0_g, across_g.at[0], across0_g),
        (pair_g.at[3], above1_g, across_g.at[1], across1_g),
    )
    for i in (3, 2, 1, 0):
        units = slice(i * half, (i + 1) * half)
        near, near_hbm, far, far_hbm = targets[i]
        for base, left, source in ((0, second_turned, grads), (half, turned, hidden)):
            total = dot(left[...], source[:, units])
            near[:, base : base + half] = total[:half].astype(near.dtype)
            far[:, base : base + half] = total[half:].astype(far.dtype)
        put(near, near_hbm)
        put(far, far_hbm)
    total = dot(hidden[...], down[...])
    result[...] = total[:piece]
    result_send[...] = total[piece:].astype(bf16)
    put(result, result_hbm)
    put(result_send, result_send_hbm)
    for copy in pending:
        copy.wait()


def unit_layer(place, params, bias, inputs, blocks):
    span, width = inputs[0].shape
    half = width // 2
    hid = blocks[0].shape[0]
    message, total = struct(bf16, half, hid), struct(f32, half, hid)
    shapes = (
        struct(f32, span, width), struct(f32, span, width),
        *[struct(bf16, span // 4, width)] * 4,
        total, total, *[message] * 6,
        struct(f32, half, width), struct(bf16, half, width), struct(f32, 1, 2 * hid),
    )
    scratch = (
        pltpu.VMEM((span, width), f32),
        pltpu.VMEM((span, width), bf16),
        pltpu.VMEM((span, width), bf16),
        pltpu.VMEM((span, width), bf16),
        pltpu.VMEM((width, span), bf16),
        pltpu.VMEM((width, 2 * hid), bf16),
        pltpu.VMEM((2 * hid, width), bf16),
        pltpu.VMEM((span, width), bf16),
        pltpu.VMEM((width, span), bf16),
        pltpu.VMEM((span, 2 * hid), bf16),
        pltpu.VMEM((span, 2 * hid), bf16),
        pltpu.VMEM((span, width), f32),
        pltpu.VMEM((span, width), f32),
        pltpu.VMEM((span, width), bf16),
        pltpu.VMEM((2, half, hid), f32),
        pltpu.VMEM((4, half, hid), bf16),
        pltpu.VMEM((2, half, hid), bf16),
        pltpu.VMEM((half, width), f32),
        pltpu.VMEM((half, width), bf16),
        pltpu.SemaphoreType.DMA((len(inputs) + 2 * len(blocks),)),
        pltpu.SemaphoreType.DMA((len(shapes) - 1,)),
    )
    return call(
        unit_kernel, "units", place, (params, bias, *inputs, *blocks), shapes, scratch,
        spaces=(
            [VECTOR] * 2 + [ANYWHERE] * (len(inputs) + len(blocks)),
            [ANYWHERE] * (len(shapes) - 1) + [VECTOR],
        ),
    )


def out_back_kernel(
    place_ref, back_ref, got0, got1, got2, got3, middle_ref, upstream_ref, params_ref, weight_ref,
    att_keep_ref, att_got_ref, own_ref, send_ref, grad_keep_ref, grad_send_ref, weight_own_ref, weight_send_ref, sums_ref,
    weight_sum,
):
    step = pl.program_id(0)
    lined = place_ref[0] == place_ref[1]
    half = own_ref.shape[1]
    part = att_keep_ref.shape[1]
    normed, inverse = layer_norm(middle_ref[...])
    got = jnp.where(
        step < 2,
        jnp.where(step == 0, got2[...], got3[...]),
        jnp.where(step == 2, got0[...], got1[...]),
    )
    back = back_ref[...] + got.astype(f32)
    grad = upstream_ref[...].astype(f32) + norm_back(back, normed, inverse, params_ref[2:3])
    rounded = grad.astype(bf16)
    values = dot_rt(rounded, weight_ref[...]).astype(bf16)
    here, there = values[:, :part], values[:, part:]
    grad_keep_ref[...] = jnp.where(lined, here, there)
    grad_send_ref[...] = jnp.where(lined, there, here)
    keep, got = att_keep_ref[...], att_got_ref[...]
    att = cat((jnp.where(lined, keep, got), jnp.where(lined, got, keep)), 1)
    total = dot_lt(rounded, att)

    @pl.when(step == 0)
    def _():
        weight_sum[...] = total
        sums_ref[...] = jnp.zeros_like(sums_ref)

    @pl.when(step > 0)
    def _():
        weight_sum[...] += total

    @pl.when(step < pl.num_programs(0) // 2)
    def _():
        own_ref[...] = grad[:, :half]
        send_ref[...] = rounded[:, half:]
        sums_ref[0:1] += jnp.sum(back * normed, axis=0, keepdims=True)
        sums_ref[1:2] += jnp.sum(back, axis=0, keepdims=True)
        sums_ref[2:3] += jnp.sum(rounded.astype(f32), axis=0, keepdims=True)

    @pl.when(step == pl.num_programs(0) - 1)
    def _():
        weight_own_ref[...] = weight_sum[:half]
        weight_send_ref[...] = weight_sum[half:].astype(bf16)


def out_back(place, back, got, middle, upstream, params, weight, att_keep, att_got):
    span, width = back.shape
    half = width // 2
    part = att_keep.shape[1]
    steps = 4
    rows = span // steps
    tile = lambda n: pl.BlockSpec((rows, n), lambda i: (i, 0))
    first = lambda n: pl.BlockSpec((rows, n), lambda i: (jnp.minimum(i, steps // 2 - 1), 0))
    return pl.pallas_call(
        out_back_kernel,
        name="out_back",
        grid=(steps,),
        in_specs=[
            SCALARS, tile(width), *[whole(v.shape) for v in got], tile(width), tile(width), whole(params.shape),
            whole(weight.shape), tile(part), tile(part),
        ],
        out_specs=[
            first(half), first(half), tile(part), tile(part),
            whole((half, 2 * part)), whole((half, 2 * part)), whole((8, width)),
        ],
        out_shape=[
            struct(f32, span // 2, half),
            struct(bf16, span // 2, half),
            struct(bf16, span, part),
            struct(bf16, span, part),
            struct(f32, half, 2 * part),
            struct(bf16, half, 2 * part),
            struct(f32, 8, width),
        ],
        scratch_shapes=[pltpu.VMEM((width, 2 * part), f32)],
        compiler_params=pltpu.CompilerParams(vmem_limit_bytes=40 * 2**20),
        cost_estimate=COST,
    )(place, back, *got, middle, upstream, params, weight, att_keep, att_got)


def result_kernel(place_ref, own_ref, got_ref, middle_ref, params_ref, keep_ref, send_ref):
    piece, half = keep_ref.shape
    total = own_ref[...] + got_ref[...].astype(f32) + params_ref[5:6]
    result = (middle_ref[:piece] + total).astype(bf16)
    keep_ref[...] = result[:, :half]
    send_ref[...] = result[:, half:]


def first_back_kernel(place_ref, grad_ref, keep_ref, got_ref, own_ref, send_ref):
    c = place_ref[2]
    span = own_ref.shape[0]
    for target, core in ((send_ref, 1 - c), (own_ref, c)):
        rows = pl.ds(pl.multiple_of(core * span, span), span)
        grads = grad_ref[rows, :]
        both = cat((dot_rt(grads, keep_ref[...]), dot_rt(grads, got_ref[...])), 1)
        target[...] = both.astype(target.dtype)


def row_sums(value):
    return cat((value, jnp.zeros((value.shape[0], 126), f32)), 1).T[:8]


def first_sum_kernel(
    place_ref, part_ref, got_ref, left_ref, right_ref, params_ref,
    own_ref, send_ref, sums_ref, param_sums_ref,
):
    half = own_ref.shape[1]
    grad = part_ref[...] + got_ref[...].astype(f32)
    own_ref[...] = grad[:, :half]
    send_ref[...] = grad[:, half:].astype(bf16)
    normed, _ = layer_norm(cat((left_ref[...], right_ref[...]), 1).astype(f32))
    scaled = grad * params_ref[0:1]
    param_sums_ref[0:1] = jnp.sum(grad * normed, axis=0, keepdims=True)
    param_sums_ref[1:2] = jnp.sum(grad, axis=0, keepdims=True)
    sums_ref[...] = row_sums(
        cat(
            (
                jnp.sum(scaled, axis=1, keepdims=True),
                jnp.sum(scaled * normed, axis=1, keepdims=True),
            ),
            1,
        )
    )


def input_kernel(
    place_ref, own_ref, got_ref, sums_ref, sums_got_ref, left_ref, right_ref, params_ref,
    mid_keep_ref, mid_got_ref, grad_ref,
):
    x = place_ref[0]
    span, half = own_ref.shape
    piece = span // 2
    normed, inverse = layer_norm(cat((left_ref[...], right_ref[...]), 1).astype(f32))
    normed = normed[:, :half]
    grad = own_ref[...] + got_ref[...].astype(f32)
    sums = (sums_ref[...] + sums_got_ref[...]) * (1.0 / (2 * half))
    sums = cat((sums, jnp.zeros((120, span), f32)), 0).T
    scaled = grad * params_ref[0:1, :half]
    grad_ref[...] = inverse * (scaled - sums[:, 0:1] - normed * sums[:, 1:2])
    rows = pl.ds(pl.multiple_of(x * piece, piece), piece)
    grad_ref[rows, :] += mid_keep_ref[...]
    rows = pl.ds(pl.multiple_of((1 - x) * piece, piece), piece)
    grad_ref[rows, :] += mid_got_ref[...].astype(f32)


def sum_dp(value):
    return lax.psum_scatter(value.astype(bf16), "dp", scatter_dimension=0, tiled=True).astype(f32)


def local(
    tokens,
    query_weight,
    key_weight,
    value_weight,
    query_bias,
    value_bias,
    out_weight,
    out_bias,
    up_weight,
    up_bias,
    down_weight,
    down_bias,
    attn_gain,
    attn_shift,
    mlp_gain,
    mlp_shift,
    cotangent,
):
    x = lax.axis_index("col")
    row = lax.axis_index("row")
    y, c = row // 2, row % 2
    z = lax.axis_index("dp")
    n_dp = lax.axis_size("dp")
    lined = x == y
    where = jnp.stack((x, y, c, z % 2)).astype(jnp.int32)
    span, half = tokens.shape
    piece = span // 2
    width = 2 * half
    length = 2 * span
    part = query_weight.shape[1]
    hid = up_weight.shape[1]

    def pick(first, second):
        return jnp.where(lined, first, second), jnp.where(lined, second, first)

    other_tokens = swap_x(tokens)
    (qkv_own,) = call(
        pack_qkv_kernel,
        "pack_qkv",
        where,
        (query_weight, key_weight, value_weight),
        (struct(bf16, half, 3 * part),),
        scratch=(pltpu.VMEM((3, half, part), bf16), pltpu.SemaphoreType.DMA((3,))),
        spaces=([ANYWHERE] * 3, [VECTOR]),
    )
    qkv_other = swap_y(qkv_own)
    core_tokens = swap_c(tokens)
    core_other = swap_c(other_tokens)
    qkv_keep, qkv_send = pick(qkv_own, qkv_other)
    qkv_got = swap_x(qkv_send)
    params = jnp.stack((attn_gain, attn_shift, mlp_gain, mlp_shift, out_bias, down_bias))
    params = cat((params, jnp.zeros((2, half), f32)), 0)
    params = cat((params, swap_x(params)), 1)
    by_unit = cat((query_bias, value_bias, up_bias), 0)
    by_unit_other = swap_y(by_unit)
    unit_keep, _ = pick(by_unit, by_unit_other)
    qkv_bias = cat((unit_keep[:part], jnp.zeros((part,), f32), unit_keep[part : 2 * part]), 0)[None]
    up_bias_all = cat((by_unit[2 * part :], by_unit_other[2 * part :]), 0)[None]

    own0, own1, cot_keep, cot_send, cot_sum = call(
        pack_kernel,
        "pack",
        where,
        (up_weight, down_weight, cotangent),
        (
            struct(bf16, hid, half), struct(bf16, hid, half),
            struct(bf16, piece, half), struct(bf16, piece, half), struct(f32, 1, half),
        ),
    )
    own0_y, own1_y, out_y, _ = lax.optimization_barrier((own0, own1, out_weight, qkv_other))
    above0, above1 = swap_y(own0_y), swap_y(own1_y)
    out_pair = cat((out_weight, swap_y(out_y)), 0)

    first_all, first_turned, chip = call(
        first_norm_kernel,
        "first_norm",
        where,
        (tokens, other_tokens, core_tokens, core_other, params),
        (struct(bf16, length, width), struct(bf16, width, length), struct(bf16, span, width)),
    )
    own0_x, out_x, qkv_got, first_all = lax.optimization_barrier((own0, out_pair, qkv_got, first_all))
    beside0, out_other = swap_x(own0_x), swap_x(out_x)
    qkv, att_keep, att_send, logsum = attend(where, first_all, qkv_keep, qkv_got, qkv_bias)
    att_send, cot_send, beside0, above1 = lax.optimization_barrier((att_send, cot_send, beside0, above1))
    att_got = swap_x(att_send)
    beside1 = swap_z(beside0)
    across0, across1 = swap_y(beside0), swap_x(above1)
    blocks = (own0, own1, beside0, beside1, above0, above1, across0, across1)
    cot_got = swap_x(cot_send)
    cot_pieces = (cot_keep, cot_got, swap_c(cot_keep), swap_c(cot_got))
    upstream, upstream_turned = call(
        upstream_kernel,
        "upstream",
        where,
        cot_pieces,
        (struct(bf16, span, width), struct(bf16, width, span)),
    )
    att_got, out_other = lax.optimization_barrier((att_got, out_other))
    out_all = cat((out_pair, out_other), 1)
    out_sum, *out_send = call(
        out_kernel,
        "out_projection",
        where,
        (att_keep, att_got, out_all),
        (struct(f32, span, width), *[struct(bf16, span // 4, width)] * 4),
        cost=LONG,
    )
    out_got = [swap_c(v) for v in out_send]
    (
        middle, back, *back_send,
        own0_g, own1_g, beside0_g, beside1_g, above0_g, above1_g, across0_g, across1_g,
        result_own, result_send, up_bias_sum,
    ) = unit_layer(
        where, params, up_bias_all, (out_sum, *out_got, chip, upstream, upstream_turned), blocks
    )
    back_got = [swap_c(v) for v in back_send]
    across0_got, across1_got = swap_y(across0_g), swap_x(across1_g)

    (
        mid_keep, mid_send, grad_keep, grad_send, out_own_g, out_send_g, second_sums,
    ) = out_back(where, back, back_got, middle, upstream, params, out_all, att_keep, att_got)
    second_sums = second_sums[:3]
    grad_got = swap_x(grad_send)
    above0_g, beside1_g, across0_got, across1_got, grad_got, out_send_g = lax.optimization_barrier(
        (above0_g, beside1_g, across0_got, across1_got, grad_got, out_send_g)
    )
    out_got_g = swap_x(out_send_g)
    beside0_got = swap_x((beside0_g + across0_got.astype(f32)).astype(bf16))
    above1_got = swap_y((above1_g + across1_got.astype(f32)).astype(bf16))
    above0_got, beside1_got = swap_y(above0_g), swap_x(beside1_g)
    qkv_grad, qkv_own_g, qkv_send_g, qkv_bias_sum = attend_back(
        where, qkv, logsum, grad_keep, grad_got, first_turned
    )
    qkv_got_g = swap_x(qkv_send_g)

    qkv_got_g, out_got_g, beside0_got, beside1_got, above0_got, above1_got = lax.optimization_barrier(
        (qkv_got_g, out_got_g, beside0_got, beside1_got, above0_got, above1_got)
    )
    late = sum_dp(
        cat(
            (
                own0_g + beside0_got.astype(f32) + above0_got.astype(f32),
                own1_g + beside1_got.astype(f32) + above1_got.astype(f32),
            ),
            1,
        )
    )
    step = hid // 2
    up_w_grad = cat((late[:, :step], late[:, hid : hid + step]), 1)
    down_w_grad = cat((late[:, step:hid], late[:, hid + step :]), 1).T
    out_pair_g = out_own_g + out_got_g.astype(f32)

    part_own, part_send = call(
        first_back_kernel,
        "first_back",
        where,
        (qkv_grad, qkv_keep, qkv_got),
        (struct(f32, span, width), struct(bf16, span, width)),
    )
    first_own, first_send, first_sums, attn_sums = call(
        first_sum_kernel,
        "first_sum",
        where,
        (part_own, swap_c(part_send), tokens, other_tokens, params),
        (
            struct(f32, span, half), struct(bf16, span, half), struct(f32, 8, span),
            struct(f32, 8, width),
        ),
    )
    mid_send, qkv_got_g = lax.optimization_barrier((mid_send, qkv_got_g))
    mid_got = swap_x(mid_send)
    first_got = swap_x(first_send)
    (input_grad,) = call(
        input_kernel,
        "input_grad",
        where,
        (
            first_own, first_got, first_sums, swap_x(first_sums), tokens, other_tokens,
            params, mid_keep, mid_got,
        ),
        (struct(f32, span, half),),
    )
    g_keep, g_send = pick(qkv_own_g, qkv_got_g.astype(f32))
    att_got_g = swap_y(cat((g_send, out_pair_g[:, part:]), 1).astype(bf16)).astype(f32)
    att_w_grad = sum_dp(cat((g_keep, out_pair_g[:, :part]), 1) + att_got_g)
    qkv_w_grad = att_w_grad[:, : 3 * part]
    out_w_grad = att_w_grad[:, 3 * part :].T

    keep, send = call(
        result_kernel,
        "result",
        where,
        (result_own, swap_c(result_send), middle, params),
        (struct(bf16, piece, half), struct(bf16, piece, half)),
    )
    send, first_got = lax.optimization_barrier((send, first_got))
    got = swap_x(send)
    outputs = cat(
        (jnp.where(x == 0, keep, got), jnp.where(x == 0, got, keep)), 0
    )

    sums = cat((second_sums, attn_sums[:2]), 0)
    from_x = swap_x(cat((up_bias_sum[0], qkv_bias_sum[0], sums[:, half:].reshape(-1)), 0))
    up_b = up_bias_sum[0] + from_x[: 2 * hid]
    b_keep, b_send = pick(qkv_bias_sum[0], from_x[2 * hid : 2 * hid + 3 * part])
    by_feature = cat(
        (
            sums[:, :half].reshape(-1) + from_x[2 * hid + 3 * part :],
            cot_sum[0],
        ),
        0,
    )
    from_y = swap_y(cat((up_b[hid:], b_send, by_feature), 0))
    small = cat((up_b[:hid], b_keep, by_feature), 0) + from_y
    units = hid + 3 * part
    small = cat((small[:units], small[units:] + swap_c(small[units:])), 0)
    small, first_got = lax.optimization_barrier((small, first_got))
    step = 1
    while step < n_dp:
        small = small + lax.ppermute(small, "dp", [(i, i ^ step) for i in range(n_dp)])
        step *= 2

    def take(base, size):
        chunk = size // n_dp
        return lax.dynamic_slice(small, (base + z * chunk,), (chunk,))

    return (
        outputs,
        input_grad,
        qkv_w_grad[:, :part],
        qkv_w_grad[:, part : 2 * part],
        qkv_w_grad[:, 2 * part :],
        take(hid, part),
        take(hid + 2 * part, part),
        out_w_grad,
        take(units + 2 * half, half),
        up_w_grad,
        take(0, hid),
        down_w_grad,
        take(units + 5 * half, half),
        take(units + 3 * half, half),
        take(units + 4 * half, half),
        take(units, half),
        take(units + half, half),
    )


def solution(mesh):
    placed = (
        P(("dp", "row"), "col"),
        P("col", "row"),
        P("col", "row"),
        P("col", "row"),
        P("row"),
        P("row"),
        P("row", "col"),
        P("col"),
        P("col", "row"),
        P("row"),
        P("row", "col"),
        P("col"),
        P("col"),
        P("col"),
        P("col"),
        P("col"),
        P(("dp", "row"), "col"),
    )
    return jax.shard_map(
        local,
        mesh=mesh,
        in_specs=placed,
        out_specs=(
            P(("dp", "row"), "col"),
            P(("dp", "row"), "col"),
            P(("col", "dp"), "row"),
            P(("col", "dp"), "row"),
            P(("col", "dp"), "row"),
            P(("row", "dp")),
            P(("row", "dp")),
            P("row", ("col", "dp")),
            P(("col", "dp")),
            P(("col", "dp"), "row"),
            P(("row", "dp")),
            P("row", ("col", "dp")),
            P(("col", "dp")),
            P(("col", "dp")),
            P(("col", "dp")),
            P(("col", "dp")),
            P(("col", "dp")),
        ),
        check_vma=False,
    )
```

```python
import functools
import jax
import jax.numpy as jnp
from jax import lax
from jax.experimental import pallas as pl
from jax.experimental.pallas import tpu as pltpu
from jax.sharding import PartitionSpec as P

HD = 64
QB = 256
QF = 384
EPS = 1e-05
bf16 = jnp.bfloat16
f32 = jnp.float32


def swap_y(value):
    return lax.ppermute(value, "row", [(r, r ^ 2) for r in range(lax.axis_size("row"))])


def swap_c(value):
    return lax.ppermute(value, "row", [(r, r ^ 1) for r in range(lax.axis_size("row"))])


def swap_x(value):
    return lax.ppermute(value, "col", [(i, i ^ 1) for i in range(lax.axis_size("col"))])


def swap_z(value):
    return lax.ppermute(value, "dp", [(i, i ^ 1) for i in range(lax.axis_size("dp"))])


def dot(left, right):
    return jnp.dot(left, right, preferred_element_type=f32)


def dot_rt(left, right):
    return lax.dot_general(left, right, (((1,), (1,)), ((), ())), preferred_element_type=f32)


def dot_lt(left, right):
    return lax.dot_general(left, right, (((0,), (0,)), ((), ())), preferred_element_type=f32)


def causal(scores):
    rows = lax.broadcasted_iota(jnp.int32, scores.shape, 0)
    cols = lax.broadcasted_iota(jnp.int32, scores.shape, 1)
    return jnp.where(cols <= rows, scores, -1e30)


def split_heads(source, target, count, scaled):
    for i in range(count):
        part = source[:, HD * i : HD * (i + 1)]
        target[i] = part * jnp.asarray(HD**-0.5, part.dtype) if i < scaled else part


def forward_kernel(
    heads, place_ref, in_ref, keep_ref, got_ref, bias_ref,
    qkv_ref, own_ref, send_ref, log_ref, wide_ref, weight, qkv,
):
    length = qkv_ref.shape[0]
    half = keep_ref.shape[0]
    weight[:half] = keep_ref[...]
    weight[half:] = got_ref[...]
    qkv_ref[...] = (dot(in_ref[...], weight[...]) + bias_ref[...]).astype(bf16)
    split_heads(qkv_ref, qkv, 3 * heads, heads)

    for low in range(0, length, QF):
        high = low + QF
        scores = []
        for head in range(heads):
            query = qkv[head, low:high, :]
            last = causal(dot_rt(query, qkv[heads + head, low:high, :]))
            scores.append((last, dot_rt(query, qkv[heads + head, 0:low, :]) if low else None))
        logs, outs = [], []
        for head, (last, first) in enumerate(scores):
            top = jnp.max(last, axis=1, keepdims=True)
            if low:
                top = jnp.maximum(top, jnp.max(first, axis=1, keepdims=True))
                first = jnp.exp(first - top)
            last = jnp.exp(last - top)
            total = jnp.sum(last, axis=1, keepdims=True)
            if low:
                total = total + jnp.sum(first, axis=1, keepdims=True)
            inverse = 1.0 / total
            out = dot((last * inverse).astype(bf16), qkv[2 * heads + head, low:high, :])
            if low:
                out = out + dot((first * inverse).astype(bf16), qkv[2 * heads + head, 0:low, :])
            outs.append(out)
            logs.append(top + jnp.log(total))
        wide_ref[low:high, :] = cat(outs, 1)
        log_ref[low:high, :] = cat(logs, 1)

    piece = length // 4
    x, c = place_ref[0], place_ref[2]
    for target, col in ((own_ref, x), (send_ref, 1 - x)):
        for i, core in enumerate((c, 1 - c)):
            start = pl.multiple_of((2 * core + col) * piece, piece)
            target[i * piece : (i + 1) * piece, :] = wide_ref[pl.ds(start, piece), :].astype(bf16)


def backward_kernel(
    heads, place_ref, qkv_ref, log_ref, wide_ref, keep_ref, got_ref, turned_ref, extra_ref,
    grad_ref, own_ref, send_ref, bias_ref,
    qkv, ups, dots, grads, key_sum, value_sum,
):
    length = qkv_ref.shape[0]
    split_heads(qkv_ref, qkv, 3 * heads, heads)
    piece = length // 4
    x, c = place_ref[0], place_ref[2]
    for source, col in ((keep_ref, x), (got_ref, 1 - x)):
        for i, core in enumerate((c, 1 - c)):
            start = pl.multiple_of((2 * core + col) * piece, piece)
            values = source[i * piece : (i + 1) * piece, :]
            wide = wide_ref[pl.ds(start, piece), :] * values.astype(f32)
            for j in range(heads):
                ups[j, pl.ds(start, piece), :] = values[:, j * HD : (j + 1) * HD]
                dots[j, pl.ds(start, piece), :] = jnp.sum(
                    wide[:, j * HD : (j + 1) * HD], axis=1, keepdims=True
                )

    key_sum[...] = jnp.zeros_like(key_sum)
    value_sum[...] = jnp.zeros_like(value_sum)
    for low in range(0, length, QB):
        high = low + QB
        sums = [0.0] * heads
        spans = [(low, high)] + ([(0, low)] if low else [])
        for start, stop in spans:
            first = []
            for head in range(heads):
                scores = dot_rt(qkv[head, low:high, :], qkv[heads + head, start:stop, :])
                if start == low:
                    scores = causal(scores)
                first.append((scores, dot_rt(ups[head, low:high, :], qkv[2 * heads + head, start:stop, :])))
            for head in range(heads):
                query = qkv[head, low:high, :]
                up = ups[head, low:high, :]
                key = qkv[heads + head, start:stop, :]
                scores, prob_grad = first[head]
                probs = jnp.exp(scores - log_ref[low:high, head : head + 1])
                score_grad = (probs * (prob_grad - dots[head, low:high, :])).astype(bf16)
                value_sum[head, :, start:stop] += dot_lt(up, probs.astype(bf16))
                key_sum[head, :, start:stop] += dot_lt(query, score_grad)
                sums[head] = sums[head] + dot(score_grad, key)
        for head in range(heads):
            grads[head, low:high, :] = (sums[head] * HD**-0.5).astype(bf16)
    for head in range(heads):
        grads[heads + head] = key_sum[head].T.astype(bf16)
        grads[2 * heads + head] = value_sum[head].T.astype(bf16)
    half = own_ref.shape[0]
    grad_ref[...] = cat([grads[i] for i in range(3 * heads)], 1)
    total = dot(turned_ref[...], grad_ref[...])
    own_ref[...] = total[:half]
    send_ref[:, : total.shape[1]] = total[half:].astype(bf16)
    end = total.shape[1] + extra_ref.shape[1]
    send_ref[:, total.shape[1] : end] = extra_ref[...]
    send_ref[:, end:] = jnp.zeros((half, send_ref.shape[1] - end), bf16)
    bias_ref[...] = jnp.sum(grad_ref[...].astype(f32), axis=0, keepdims=True)


def whole(shape):
    return pl.BlockSpec(shape, lambda head: (0,) * len(shape))


COST = pl.CostEstimate(flops=1, bytes_accessed=1, transcendentals=0)
LONG = pl.CostEstimate(flops=4 * 10**10, bytes_accessed=1, transcendentals=0)
SCALARS = pl.BlockSpec(memory_space=pltpu.SMEM)


def struct(dtype, *shape):
    return jax.ShapeDtypeStruct(shape, dtype)


def attend(place, first_all, keep, got, bias):
    length = first_all.shape[0]
    width = keep.shape[1]
    heads = width // (3 * HD)
    shapes = [
        struct(bf16, length, width),
        struct(bf16, length // 2, heads * HD),
        struct(bf16, length // 2, heads * HD),
        struct(f32, length, heads),
        struct(f32, length, heads * HD),
    ]
    return pl.pallas_call(
        functools.partial(forward_kernel, heads),
        name="attend",
        grid=(1,),
        in_specs=[SCALARS] + [whole(v.shape) for v in (first_all, keep, got, bias)],
        out_specs=[whole(v.shape) for v in shapes],
        out_shape=shapes,
        scratch_shapes=[
            pltpu.VMEM((first_all.shape[1], width), bf16),
            pltpu.VMEM((3 * heads, length, HD), bf16),
        ],
        compiler_params=pltpu.CompilerParams(vmem_limit_bytes=48 * 2**20),
        cost_estimate=LONG,
    )(place, first_all, keep, got, bias)


def attend_back(place, qkv, log, wide, keep, got, turned, extra):
    length, width = qkv.shape
    heads = width // (3 * HD)
    half = turned.shape[0] // 2
    shapes = [
        struct(bf16, length, width),
        struct(f32, half, width),
        struct(bf16, half, -(-(width + extra.shape[1]) // 128) * 128),
        struct(f32, 1, width),
    ]
    return pl.pallas_call(
        functools.partial(backward_kernel, heads),
        name="attend_back",
        grid=(1,),
        in_specs=[SCALARS] + [whole(v.shape) for v in (qkv, log, wide, keep, got, turned, extra)],
        out_specs=[whole(v.shape) for v in shapes],
        out_shape=shapes,
        scratch_shapes=[
            pltpu.VMEM((3 * heads, length, HD), bf16),
            pltpu.VMEM((heads, length, HD), bf16),
            pltpu.VMEM((heads, length, 1), f32),
            pltpu.VMEM((3 * heads, length, HD), bf16),
            pltpu.VMEM((heads, HD, length), f32),
            pltpu.VMEM((heads, HD, length), f32),
        ],
        compiler_params=pltpu.CompilerParams(vmem_limit_bytes=52 * 2**20),
        cost_estimate=LONG,
    )(place, qkv, log, wide, keep, got, turned, extra)


def layer_norm(values):
    center = jnp.mean(values, axis=1, keepdims=True)
    inverse = lax.rsqrt(jnp.mean(values * values, axis=1, keepdims=True) - center * center + EPS)
    return (values - center) * inverse, inverse


def norm_back(upstream, normed, inverse, gain):
    scaled = upstream * gain
    return inverse * (
        scaled
        - jnp.mean(scaled, axis=1, keepdims=True)
        - normed * jnp.mean(scaled * normed, axis=1, keepdims=True)
    )


def cat(parts, axis):
    return jnp.concatenate(parts, axis=axis)


VECTOR = pl.BlockSpec(memory_space=pltpu.VMEM)
ANYWHERE = pl.BlockSpec(memory_space=pl.ANY)


def call(kernel, name, place, inputs, shapes, scratch=(), spaces=None, cost=COST):
    ins, outs = spaces or ([VECTOR] * len(inputs), [VECTOR] * len(shapes))
    return pl.pallas_call(
        kernel,
        name=name,
        in_specs=[SCALARS] + list(ins),
        out_specs=list(outs),
        out_shape=list(shapes),
        scratch_shapes=list(scratch),
        compiler_params=pltpu.CompilerParams(vmem_limit_bytes=48 * 2**20),
        cost_estimate=cost,
    )(place, *inputs)


def first_norm_kernel(
    place_ref, own_ref, other_ref, core_own_ref, core_other_ref, params_ref,
    all_ref, turned_ref, chip_ref,
):
    x, c = place_ref[0], place_ref[2]
    span = own_ref.shape[0]
    piece = span // 2
    for i, (left, right) in enumerate(((own_ref, other_ref), (core_own_ref, core_other_ref))):
        start = pl.multiple_of((c if i == 0 else 1 - c) * span, span)
        values = cat((left[...], right[...]), 1).astype(f32)
        normed, _ = layer_norm(values)
        rounded = (normed * params_ref[0:1] + params_ref[1:2]).astype(bf16)
        all_ref[pl.ds(start, span), :] = rounded
        turned_ref[:, pl.ds(start, span)] = rounded.T
        rows = pl.ds(pl.multiple_of(x * piece, piece), piece)
        chip_ref[i * piece : (i + 1) * piece, :] = cat((left[rows, :], right[rows, :]), 1)


def upstream_kernel(place_ref, own_ref, side_ref, core_ref, all_ref, turned_ref):
    piece = own_ref.shape[0]
    pieces = ((own_ref, side_ref.at[piece:]), (core_ref.at[:piece], core_ref.at[piece:]))
    for i, (left, right) in enumerate(pieces):
        values = cat((left[...], right[...]), 1)
        all_ref[i * piece : (i + 1) * piece, :] = values
        turned_ref[:, i * piece : (i + 1) * piece] = values.T


def pack_qkv_kernel(place_ref, query_hbm, key_hbm, value_hbm, all_ref, parts, sems):
    copies = [
        pltpu.make_async_copy(source, parts.at[i], sems.at[i])
        for i, source in enumerate((query_hbm, key_hbm, value_hbm))
    ]
    for copy in copies:
        copy.start()
    for copy in copies:
        copy.wait()
    all_ref[...] = cat((parts[0], parts[1], parts[2]), 1)


def pack_kernel(
    place_ref, up_ref, down_ref, out_ref, cot_ref, first, second, keep_ref, send_ref, sum_ref
):
    x, lead = place_ref[0], place_ref[3]
    half = first.shape[1]
    piece = keep_ref.shape[0]
    for i, target in ((lead, first), (1 - lead, second)):
        units = pl.ds(pl.multiple_of(i * half, half), half)
        target[:half] = up_ref[:, units]
        target[half : 2 * half] = down_ref[units]
    second[2 * half :] = out_ref[...]
    for target, col in ((keep_ref, x), (send_ref, 1 - x)):
        target[...] = cot_ref[pl.ds(pl.multiple_of(col * piece, piece), piece), :]
    sum_ref[...] = jnp.sum(cot_ref[...].astype(f32), axis=0, keepdims=True)


def out_kernel(place_ref, keep_ref, got_ref, weight_ref, sum_ref, *send_refs):
    lined = place_ref[0] == place_ref[1]
    keep, got = keep_ref[...], got_ref[...]
    values = cat((jnp.where(lined, keep, got), jnp.where(lined, got, keep)), 1)
    total = dot(values, weight_ref[...])
    sum_ref[...] = total
    rows = send_refs[0].shape[0]
    for i, send_ref in enumerate(send_refs):
        send_ref[...] = total[i * rows : (i + 1) * rows].astype(bf16)


def unit_tiles(count):
    step = 512
    return [(low, min(low + step, count)) for low in range(0, count, step)]


def unit_kernel(
    place_ref, params_ref, bias_ref, sum_hbm, got0, got1, chip_hbm, upstream_hbm, turned_hbm,
    own0, own1, beside0, beside1, above0, above1, across0, across1,
    middle_hbm, back_hbm, back0, back1, own0_g, own1_g, beside_g, above_g, across0_g, across1_g,
    result_hbm, result_send_hbm, bias_sum_ref,
    sums, got, chip, upstream, turned, up, down, second, second_turned, hidden, grads,
    middle, back, back_send, own_g, pair_g, across_g, result, result_send, in_sems, out_sems,
):
    lead = place_ref[3]
    half = own0.shape[1]
    rows = piece = got0.shape[0]
    started, pending = [], []

    def fetch(source, target):
        copy = pltpu.make_async_copy(source, target, in_sems.at[len(started)])
        copy.start()
        started.append(copy)
        return copy

    def put(source, target):
        copy = pltpu.make_async_copy(source, target, out_sems.at[len(pending)])
        copy.start()
        pending.append(copy)

    first = [fetch(sum_hbm, sums), fetch(chip_hbm, chip)]
    for i, source in enumerate((got0, got1)):
        first.append(fetch(source, got.at[pl.ds((1 - i) * rows, rows)]))
    ups, downs = [], []
    for base, left, right in ((0, (own0, own1), (beside0, beside1)), (2, (above0, above1), (across0, across1))):
        for i in range(2):
            number = base + (lead if i == 0 else 1 - lead)
            units = pl.ds(pl.multiple_of(number * half, half), half)
            for j, source in enumerate((left[i], right[i])):
                features = pl.ds(j * half, half)
                ups.append(fetch(source.at[pl.ds(0, half)], up.at[features, units]))
                downs.append(fetch(source.at[pl.ds(half, half)], down.at[units, features]))
    downs.append(fetch(upstream_hbm, upstream))
    later = fetch(turned_hbm, turned)

    for copy in first:
        copy.wait()
    middle[...] = chip[...].astype(f32) + (sums[...] + got[...].astype(f32) + params_ref[4:5])
    put(middle, middle_hbm)
    normed, _ = layer_norm(middle[...])
    second[...] = (normed * params_ref[2:3] + params_ref[3:4]).astype(bf16)
    for copy in ups + downs:
        copy.wait()
    root = 0.7978845608028654
    total = None
    for low, high in unit_tiles(up.shape[1]):
        pre = dot(second[...], up[:, low:high]) + bias_ref[:, low:high]
        square = pre * pre
        curve = jnp.tanh(root * (pre + 0.044715 * (square * pre)))
        share = 0.5 * (1.0 + curve)
        hidden[:, low:high] = (pre * share).astype(bf16)
        slope = share + (0.5 * root) * pre * (1.0 - curve * curve) * (1.0 + 0.134145 * square)
        grad = (dot_rt(upstream[...], down[low:high, :]) * slope).astype(bf16)
        grads[:, low:high] = grad
        bias_sum_ref[:, low:high] = jnp.sum(grad.astype(f32), axis=0, keepdims=True)
        part = dot_rt(grad, up[:, low:high])
        total = part if total is None else total + part
    back[...] = total
    back_send[...] = total.astype(bf16)
    put(back, back_hbm)
    for i, target in enumerate((back0, back1)):
        put(back_send.at[pl.ds(i * rows, rows)], target)

    second_turned[...] = second[...].T
    later.wait()
    targets = (
        (own_g.at[0], own0_g, pair_g.at[0], beside_g.at[0]),
        (own_g.at[1], own1_g, pair_g.at[1], beside_g.at[1]),
        (pair_g.at[2], above_g.at[0], across_g.at[0], across0_g),
        (pair_g.at[3], above_g.at[1], across_g.at[1], across1_g),
    )
    for i in (3, 2, 1, 0):
        units = slice(i * half, (i + 1) * half)
        near, near_hbm, far, far_hbm = targets[i]
        for base, left, source in ((0, second_turned, grads), (half, turned, hidden)):
            total = dot(left[...], source[:, units])
            near[:, base : base + half] = total[:half].astype(near.dtype)
            far[:, base : base + half] = total[half:].astype(far.dtype)
        put(near, near_hbm)
        put(far, far_hbm)
    total = dot(hidden[...], down[...])
    result[...] = total[:piece]
    result_send[...] = total[piece:].astype(bf16)
    put(result, result_hbm)
    put(result_send, result_send_hbm)
    for copy in pending:
        copy.wait()


def unit_layer(place, params, bias, inputs, blocks):
    span, width = inputs[0].shape
    half = width // 2
    hid = blocks[0].shape[0]
    message, total = struct(bf16, half, hid), struct(f32, half, hid)
    shapes = (
        struct(f32, span, width), struct(f32, span, width),
        *[struct(bf16, span // 2, width)] * 2,
        total, total, struct(bf16, 2, half, hid), struct(bf16, 2, half, hid), message, message,
        struct(f32, half, width), struct(bf16, half, width), struct(f32, 1, 2 * hid),
    )
    scratch = (
        pltpu.VMEM((span, width), f32),
        pltpu.VMEM((span, width), bf16),
        pltpu.VMEM((span, width), bf16),
        pltpu.VMEM((span, width), bf16),
        pltpu.VMEM((width, span), bf16),
        pltpu.VMEM((width, 2 * hid), bf16),
        pltpu.VMEM((2 * hid, width), bf16),
        pltpu.VMEM((span, width), bf16),
        pltpu.VMEM((width, span), bf16),
        pltpu.VMEM((span, 2 * hid), bf16),
        pltpu.VMEM((span, 2 * hid), bf16),
        pltpu.VMEM((span, width), f32),
        pltpu.VMEM((span, width), f32),
        pltpu.VMEM((span, width), bf16),
        pltpu.VMEM((2, half, hid), f32),
        pltpu.VMEM((4, half, hid), bf16),
        pltpu.VMEM((2, half, hid), bf16),
        pltpu.VMEM((half, width), f32),
        pltpu.VMEM((half, width), bf16),
        pltpu.SemaphoreType.DMA((len(inputs) + 2 * len(blocks),)),
        pltpu.SemaphoreType.DMA((len(shapes) + 1,)),
    )
    return call(
        unit_kernel, "units", place, (params, bias, *inputs, *blocks), shapes, scratch,
        spaces=(
            [VECTOR] * 2 + [ANYWHERE] * (len(inputs) + len(blocks)),
            [ANYWHERE] * (len(shapes) - 1) + [VECTOR],
        ),
    )


def out_back_kernel(
    place_ref, back_ref, got0, got1, middle_ref, upstream_ref, params_ref, weight_ref,
    att_keep_ref, att_got_ref, own_ref, send_ref, grad_keep_ref, grad_send_ref, weight_own_ref, weight_send_ref, sums_ref,
    weight_sum,
):
    step = pl.program_id(0)
    lined = place_ref[0] == place_ref[1]
    half = own_ref.shape[1]
    part = att_keep_ref.shape[1]
    normed, inverse = layer_norm(middle_ref[...])
    rows = back_ref.shape[0]
    rows = pl.ds(pl.multiple_of(lax.rem(step, 2) * rows, rows), rows)
    got = jnp.where(step < 2, got1[rows, :], got0[rows, :])
    back = back_ref[...] + got.astype(f32)
    grad = upstream_ref[...].astype(f32) + norm_back(back, normed, inverse, params_ref[2:3])
    rounded = grad.astype(bf16)
    values = dot_rt(rounded, weight_ref[...]).astype(bf16)
    here, there = values[:, :part], values[:, part:]
    grad_keep_ref[...] = jnp.where(lined, here, there)
    grad_send_ref[...] = jnp.where(lined, there, here)
    keep, got = att_keep_ref[...], att_got_ref[...]
    att = cat((jnp.where(lined, keep, got), jnp.where(lined, got, keep)), 1)
    total = dot_lt(rounded, att)

    @pl.when(step == 0)
    def _():
        weight_sum[...] = total
        sums_ref[...] = jnp.zeros_like(sums_ref)

    @pl.when(step > 0)
    def _():
        weight_sum[...] += total

    @pl.when(step < pl.num_programs(0) // 2)
    def _():
        own_ref[...] = grad[:, :half]
        send_ref[...] = rounded[:, half:]
        sums_ref[0:1] += jnp.sum(back * normed, axis=0, keepdims=True)
        sums_ref[1:2] += jnp.sum(back, axis=0, keepdims=True)
        sums_ref[2:3] += jnp.sum(rounded.astype(f32), axis=0, keepdims=True)

    @pl.when(step == pl.num_programs(0) - 1)
    def _():
        weight_own_ref[...] = weight_sum[:half]
        weight_send_ref[...] = weight_sum[half:].astype(bf16)


def out_back(place, back, got, middle, upstream, params, weight, att_keep, att_got):
    span, width = back.shape
    half = width // 2
    part = att_keep.shape[1]
    steps = 4
    rows = span // steps
    tile = lambda n: pl.BlockSpec((rows, n), lambda i: (i, 0))
    first = lambda n: pl.BlockSpec((rows, n), lambda i: (jnp.minimum(i, steps // 2 - 1), 0))
    return pl.pallas_call(
        out_back_kernel,
        name="out_back",
        grid=(steps,),
        in_specs=[
            SCALARS, tile(width), *[whole(v.shape) for v in got], tile(width), tile(width), whole(params.shape),
            whole(weight.shape), tile(part), tile(part),
        ],
        out_specs=[
            first(half), first(half), tile(part), tile(part),
            whole((half, 2 * part)), whole((half, 2 * part)), whole((8, width)),
        ],
        out_shape=[
            struct(f32, span // 2, half),
            struct(bf16, span // 2, half),
            struct(bf16, span, part),
            struct(bf16, span, part),
            struct(f32, half, 2 * part),
            struct(bf16, half, 2 * part),
            struct(f32, 8, width),
        ],
        scratch_shapes=[pltpu.VMEM((width, 2 * part), f32)],
        compiler_params=pltpu.CompilerParams(vmem_limit_bytes=52 * 2**20),
        cost_estimate=COST,
    )(place, back, *got, middle, upstream, params, weight, att_keep, att_got)


def result_kernel(place_ref, own_ref, got_ref, middle_ref, params_ref, keep_ref, send_ref):
    piece, half = keep_ref.shape
    total = own_ref[...] + got_ref[...].astype(f32) + params_ref[5:6]
    result = (middle_ref[:piece] + total).astype(bf16)
    keep_ref[...] = result[:, :half]
    send_ref[...] = result[:, half:]


def first_back_kernel(place_ref, grad_ref, keep_ref, got_ref, own_ref, send0, send1):
    c = place_ref[2]
    span = own_ref.shape[0]
    piece = span // 2
    for target, start in (
        (send0, (1 - c) * span),
        (send1, (1 - c) * span + piece),
        (own_ref.at[:piece], c * span),
        (own_ref.at[piece:], c * span + piece),
    ):
        grads = grad_ref[pl.ds(pl.multiple_of(start, piece), piece), :]
        both = cat((dot_rt(grads, keep_ref[...]), dot_rt(grads, got_ref[...])), 1)
        target[...] = both.astype(target.dtype)


def pick_kernel(place_ref, own_ref, got_ref, out_ref, keep_ref, send_ref):
    lined = place_ref[0] == place_ref[1]
    width = own_ref.shape[1]
    part = width // 3
    own, got = own_ref[...], got_ref[:, :width].astype(f32)
    out = out_ref[...] + got_ref[:, width : width + 2 * part].astype(f32)
    keep_ref[...] = cat((jnp.where(lined, own, got), out[:, :part]), 1)
    send_ref[...] = cat((jnp.where(lined, got, own), out[:, part:]), 1).astype(bf16)


def row_sums(value):
    return cat((value, jnp.zeros((value.shape[0], 126), f32)), 1).T[:8]


def first_sum_kernel(
    place_ref, part_ref, got0, got1, left_ref, right_ref, params_ref,
    own_ref, send_ref, sums_ref, param_sums_ref,
):
    half = own_ref.shape[1]
    grad = part_ref[...] + cat((got0[...], got1[...]), 0).astype(f32)
    own_ref[...] = grad[:, :half]
    send_ref[...] = grad[:, half:].astype(bf16)
    normed, _ = layer_norm(cat((left_ref[...], right_ref[...]), 1).astype(f32))
    scaled = grad * params_ref[0:1]
    param_sums_ref[0:1] = jnp.sum(grad * normed, axis=0, keepdims=True)
    param_sums_ref[1:2] = jnp.sum(grad, axis=0, keepdims=True)
    sums_ref[...] = row_sums(
        cat(
            (
                jnp.sum(scaled, axis=1, keepdims=True),
                jnp.sum(scaled * normed, axis=1, keepdims=True),
            ),
            1,
        )
    )


def input_kernel(
    place_ref, own_ref, got_ref, sums_ref, sums_got_ref, left_ref, right_ref, params_ref,
    mid_keep_ref, mid_got_ref, grad_ref,
):
    x = place_ref[0]
    span, half = own_ref.shape
    piece = span // 2
    normed, inverse = layer_norm(cat((left_ref[...], right_ref[...]), 1).astype(f32))
    normed = normed[:, :half]
    grad = own_ref[...] + got_ref[...].astype(f32)
    sums = (sums_ref[...] + sums_got_ref[...]) * (1.0 / (2 * half))
    sums = cat((sums, jnp.zeros((120, span), f32)), 0).T
    scaled = grad * params_ref[0:1, :half]
    grad_ref[...] = inverse * (scaled - sums[:, 0:1] - normed * sums[:, 1:2])
    rows = pl.ds(pl.multiple_of(x * piece, piece), piece)
    grad_ref[rows, :] += mid_keep_ref[...]
    rows = pl.ds(pl.multiple_of((1 - x) * piece, piece), piece)
    grad_ref[rows, :] += mid_got_ref[...].astype(f32)


def sum_dp(value):
    return lax.psum_scatter(value.astype(bf16), "dp", scatter_dimension=0, tiled=True).astype(f32)


def halve_dp(value, step):
    low = (lax.axis_index("dp") // step) % 2 == 0
    rows = value.shape[0] // 2
    keep = jnp.where(low, value[:rows], value[rows:])
    send = jnp.where(low, value[rows:], value[:rows]).astype(bf16)
    pairs = [(i, i ^ step) for i in range(lax.axis_size("dp"))]
    return keep + lax.ppermute(send, "dp", pairs).astype(f32)


def small_x_kernel(place_ref, unit_ref, qkv_ref, second_ref, first_ref, send_ref):
    half = send_ref.shape[1]
    part = half // 2
    send_ref[...] = jnp.zeros_like(send_ref)
    for i in range(4):
        send_ref[i : i + 1] = unit_ref[:, i * half : (i + 1) * half]
    send_ref[4:5, :part] = qkv_ref[:, :part]
    send_ref[4:5, part:] = qkv_ref[:, 2 * part : 3 * part]
    send_ref[5:8] = second_ref[0:3, half:]
    send_ref[8:10] = first_ref[0:2, half:]


def small_y_kernel(place_ref, own_ref, got_ref, second_ref, first_ref, cot_ref, keep_ref, send_ref):
    lined = place_ref[0] == place_ref[1]
    half = send_ref.shape[1]
    own, got = own_ref[...], got_ref[...]
    features = cat(
        (second_ref[0:3, :half] + got[5:8], first_ref[0:2, :half] + got[8:10], cot_ref[...]), 0
    )
    for target, units, bias in (
        (keep_ref, own[0:2] + got[0:2], jnp.where(lined, own[4:5], got[4:5])),
        (send_ref, own[2:4] + got[2:4], jnp.where(lined, got[4:5], own[4:5])),
    ):
        target[...] = jnp.zeros_like(target)
        target[0:2] = units
        target[2:3] = bias
        target[3:9] = features


def small_c_kernel(place_ref, own_ref, got_ref, sum_ref):
    sum_ref[...] = own_ref[...]
    sum_ref[3:9] += got_ref[3:9]


def local(
    tokens,
    query_weight,
    key_weight,
    value_weight,
    query_bias,
    value_bias,
    out_weight,
    out_bias,
    up_weight,
    up_bias,
    down_weight,
    down_bias,
    attn_gain,
    attn_shift,
    mlp_gain,
    mlp_shift,
    cotangent,
):
    x = lax.axis_index("col")
    row = lax.axis_index("row")
    y, c = row // 2, row % 2
    z = lax.axis_index("dp")
    n_dp = lax.axis_size("dp")
    lined = x == y
    where = jnp.stack((x, y, c, z % 2)).astype(jnp.int32)
    span, half = tokens.shape
    piece = span // 2
    width = 2 * half
    length = 2 * span
    part = query_weight.shape[1]
    hid = up_weight.shape[1]

    def pick(first, second):
        return jnp.where(lined, first, second), jnp.where(lined, second, first)

    other_tokens = swap_x(tokens)
    (qkv_own,) = call(
        pack_qkv_kernel,
        "pack_qkv",
        where,
        (query_weight, key_weight, value_weight),
        (struct(bf16, half, 3 * part),),
        scratch=(pltpu.VMEM((3, half, part), bf16), pltpu.SemaphoreType.DMA((3,))),
        spaces=([ANYWHERE] * 3, [VECTOR]),
    )
    qkv_other = swap_y(qkv_own)
    core_tokens = swap_c(tokens)
    core_other = swap_c(other_tokens)
    qkv_keep, qkv_send = pick(qkv_own, qkv_other)
    qkv_got = swap_x(qkv_send)
    params = jnp.stack((attn_gain, attn_shift, mlp_gain, mlp_shift, out_bias, down_bias))
    params = cat((params, jnp.zeros((2, half), f32)), 0)
    params = cat((params, swap_x(params)), 1)
    by_unit = cat((query_bias, value_bias, up_bias), 0)
    by_unit_other = swap_y(by_unit)
    unit_keep, _ = pick(by_unit, by_unit_other)
    qkv_bias = cat((unit_keep[:part], jnp.zeros((part,), f32), unit_keep[part : 2 * part]), 0)[None]
    up_bias_all = cat((by_unit[2 * part :], by_unit_other[2 * part :]), 0)[None]

    own0, own1, cot_keep, cot_send, cot_sum = call(
        pack_kernel,
        "pack",
        where,
        (up_weight, down_weight, out_weight, cotangent),
        (
            struct(bf16, hid, half), struct(bf16, hid + part, half),
            struct(bf16, piece, half), struct(bf16, piece, half), struct(f32, 1, half),
        ),
    )
    own0_y, own1_y, _ = lax.optimization_barrier((own0, own1, qkv_other))
    above0, above1 = swap_y(own0_y), swap_y(own1_y)
    out_pair = cat((out_weight, above1[2 * half :]), 0)

    first_all, first_turned, chip = call(
        first_norm_kernel,
        "first_norm",
        where,
        (tokens, other_tokens, core_tokens, core_other, params),
        (struct(bf16, length, width), struct(bf16, width, length), struct(bf16, span, width)),
    )
    own0_x, qkv_got, first_all = lax.optimization_barrier((own0, qkv_got, first_all))
    beside0 = swap_x(own0_x)
    side = cat((out_pair, cot_send), 0)
    qkv, att_keep, att_send, logsum, wide = attend(where, first_all, qkv_keep, qkv_got, qkv_bias)
    att_send, side, beside0, above1 = lax.optimization_barrier((att_send, side, beside0, above1))
    att_got, side, above0 = lax.optimization_barrier((swap_x(att_send), swap_x(side), above0))
    beside1 = swap_z(beside0)
    across0, across1 = swap_y(beside0), swap_x(above1[: 2 * half])
    blocks = (own0, own1, beside0, beside1, above0, above1, across0, across1)
    upstream, upstream_turned = call(
        upstream_kernel,
        "upstream",
        where,
        (cot_keep, side, swap_c(cat((cot_keep, side[half:]), 0))),
        (struct(bf16, span, width), struct(bf16, width, span)),
    )
    out_all = cat((out_pair, side[:half]), 1)
    out_sum, *out_send = call(
        out_kernel,
        "out_projection",
        where,
        (att_keep, att_got, out_all),
        (struct(f32, span, width), *[struct(bf16, span // 2, width)] * 2),
        cost=LONG,
    )
    out_got = [swap_c(v) for v in out_send]
    (
        middle, back, *back_send,
        own0_g, own1_g, beside_g, above_g, across0_g, across1_g,
        result_own, result_send, up_bias_sum,
    ) = unit_layer(
        where, params, up_bias_all, (out_sum, *out_got, chip, upstream, upstream_turned), blocks
    )
    back_got = [swap_c(v) for v in back_send]
    across0_got, across1_got = swap_y(across0_g), swap_x(across1_g)

    (
        mid_keep, mid_send, grad_keep, grad_send, out_own_g, out_send_g, second_sums,
    ) = out_back(where, back, back_got, middle, upstream, params, out_all, att_keep, att_got)
    grad_got = swap_x(grad_send)
    beside_g, above_g, across0_got, across1_got, grad_got = lax.optimization_barrier(
        (beside_g, above_g, across0_got, across1_got, grad_got)
    )
    add = lambda first, second: (first.astype(f32) + second.astype(f32)).astype(bf16)
    beside_got = swap_x(jnp.stack((add(beside_g[0], across0_got), beside_g[1])))
    above_got = swap_y(jnp.stack((above_g[0], add(above_g[1], across1_got))))
    qkv_grad, qkv_own_g, qkv_send_g, qkv_bias_sum = attend_back(
        where, qkv, logsum, wide, grad_keep, grad_got, first_turned, out_send_g
    )
    qkv_got_g = swap_x(qkv_send_g)

    part_own, *part_send = call(
        first_back_kernel,
        "first_back",
        where,
        (qkv_grad, qkv_keep, qkv_got),
        (struct(f32, span, width), *[struct(bf16, piece, width)] * 2),
    )
    first_own, first_send, first_sums, attn_sums = call(
        first_sum_kernel,
        "first_sum",
        where,
        (part_own, *[swap_c(v) for v in part_send], tokens, other_tokens, params),
        (
            struct(f32, span, half), struct(bf16, span, half), struct(f32, 8, span),
            struct(f32, 8, width),
        ),
    )
    first_got = swap_x(first_send)
    first_own, beside_got, above_got = lax.optimization_barrier((first_own, beside_got, above_got))
    others = beside_got.astype(f32) + above_got.astype(f32)
    late = cat((own0_g + others[0], own1_g + others[1]), 1).astype(bf16)
    row_shape = struct(f32, 16, half)
    (small_x,) = call(
        small_x_kernel,
        "small_x",
        where,
        (up_bias_sum, qkv_bias_sum, second_sums, attn_sums),
        (row_shape,),
    )
    late, mid_send, qkv_got_g, small_got = lax.optimization_barrier(
        (late, mid_send, qkv_got_g, swap_x(small_x))
    )
    late = sum_dp(late)
    att_keep_g, att_send_g = call(
        pick_kernel,
        "pick",
        where,
        (qkv_own_g, qkv_got_g, out_own_g),
        (struct(f32, half, 4 * part), struct(bf16, half, 4 * part)),
    )
    att_got_g = swap_y(att_send_g).astype(f32)
    small, send = call(
        small_y_kernel,
        "small_y",
        where,
        (small_x, small_got, second_sums, attn_sums, cot_sum),
        (row_shape, row_shape),
    )
    att_got_g, first_got, result_own, small_got = lax.optimization_barrier(
        (att_got_g, first_got, result_own, swap_y(send))
    )
    small = small + small_got
    (small,) = call(small_c_kernel, "small_c", where, (small, swap_c(small)), (row_shape,))
    att_w_grad = att_keep_g + att_got_g
    steps = [n_dp >> i for i in range(1, n_dp.bit_length())]
    for i, step in enumerate(steps):
        att_w_grad = halve_dp(att_w_grad, step)
        if i == 0:
            att_w_grad, late, small = lax.optimization_barrier((att_w_grad, late, small))
    for step in steps:
        small = small + lax.ppermute(small, "dp", [(i, i ^ step) for i in range(n_dp)])
    qkv_w_grad = att_w_grad[:, : 3 * part]
    out_w_grad = att_w_grad[:, 3 * part :].T
    step = hid // 2
    up_w_grad = cat((late[:, :step], late[:, hid : hid + step]), 1)
    down_w_grad = cat((late[:, step:hid], late[:, hid + step :]), 1).T

    mid_got = swap_x(mid_send)
    (input_grad,) = call(
        input_kernel,
        "input_grad",
        where,
        (
            first_own, first_got, first_sums, swap_x(first_sums), tokens, other_tokens,
            params, mid_keep, mid_got,
        ),
        (struct(f32, span, half),),
    )
    keep, send = call(
        result_kernel,
        "result",
        where,
        (result_own, swap_c(result_send), middle, params),
        (struct(bf16, piece, half), struct(bf16, piece, half)),
    )
    send, first_got = lax.optimization_barrier((send, first_got))
    got = swap_x(send)
    outputs = cat(
        (jnp.where(x == 0, keep, got), jnp.where(x == 0, got, keep)), 0
    )

    def take(value, size):
        chunk = size // n_dp
        return lax.dynamic_slice(value.reshape(-1), (z * chunk,), (chunk,))

    return (
        outputs,
        input_grad,
        qkv_w_grad[:, :part],
        qkv_w_grad[:, part : 2 * part],
        qkv_w_grad[:, 2 * part :],
        take(small[2, :part], part),
        take(small[2, part:], part),
        out_w_grad,
        take(small[5], half),
        up_w_grad,
        take(small[:2], hid),
        down_w_grad,
        take(small[8], half),
        take(small[6], half),
        take(small[7], half),
        take(small[3], half),
        take(small[4], half),
    )


def solution(mesh):
    placed = (
        P(("dp", "row"), "col"),
        P("col", "row"),
        P("col", "row"),
        P("col", "row"),
        P("row"),
        P("row"),
        P("row", "col"),
        P("col"),
        P("col", "row"),
        P("row"),
        P("row", "col"),
        P("col"),
        P("col"),
        P("col"),
        P("col"),
        P("col"),
        P(("dp", "row"), "col"),
    )
    return jax.shard_map(
        local,
        mesh=mesh,
        in_specs=placed,
        out_specs=(
            P(("dp", "row"), "col"),
            P(("dp", "row"), "col"),
            P(("col", "dp"), "row"),
            P(("col", "dp"), "row"),
            P(("col", "dp"), "row"),
            P(("row", "dp")),
            P(("row", "dp")),
            P("row", ("col", "dp")),
            P(("col", "dp")),
            P(("col", "dp"), "row"),
            P(("row", "dp")),
            P("row", ("col", "dp")),
            P(("col", "dp")),
            P(("col", "dp")),
            P(("col", "dp")),
            P(("col", "dp")),
            P(("col", "dp")),
        ),
        check_vma=False,
    )
```

```python
import functools
import jax
import jax.numpy as jnp
from jax import lax
from jax.experimental import pallas as pl
from jax.experimental.pallas import tpu as pltpu
from jax.sharding import PartitionSpec as P

HD = 64
QB = 256
QF = 384
EPS = 1e-05
bf16 = jnp.bfloat16
f32 = jnp.float32


def swap_y(value):
    return lax.ppermute(value, "row", [(r, r ^ 2) for r in range(lax.axis_size("row"))])


def swap_c(value):
    return lax.ppermute(value, "row", [(r, r ^ 1) for r in range(lax.axis_size("row"))])


def swap_x(value):
    return lax.ppermute(value, "col", [(i, i ^ 1) for i in range(lax.axis_size("col"))])


def swap_z(value):
    return lax.ppermute(value, "dp", [(i, i ^ 1) for i in range(lax.axis_size("dp"))])


def dot(left, right):
    return jnp.dot(left, right, preferred_element_type=f32)


def dot_rt(left, right):
    return lax.dot_general(left, right, (((1,), (1,)), ((), ())), preferred_element_type=f32)


def dot_lt(left, right):
    return lax.dot_general(left, right, (((0,), (0,)), ((), ())), preferred_element_type=f32)


def causal(scores):
    rows = lax.broadcasted_iota(jnp.int32, scores.shape, 0)
    cols = lax.broadcasted_iota(jnp.int32, scores.shape, 1)
    return jnp.where(cols <= rows, scores, -1e30)


def split_heads(source, target, count, scaled):
    for i in range(count):
        part = source[:, HD * i : HD * (i + 1)]
        target[i] = part * jnp.asarray(HD**-0.5, part.dtype) if i < scaled else part


def forward_kernel(
    heads, place_ref, in_ref, keep_ref, got_ref, bias_ref,
    qkv_ref, own_ref, send_ref, log_ref, wide_ref, weight, qkv,
):
    length = qkv_ref.shape[0]
    half = keep_ref.shape[0]
    weight[:half] = keep_ref[...]
    weight[half:] = got_ref[...]
    qkv_ref[...] = (dot(in_ref[...], weight[...]) + bias_ref[...]).astype(bf16)
    split_heads(qkv_ref, qkv, 3 * heads, heads)

    for low in range(0, length, QF):
        high = low + QF
        scores = []
        for head in range(heads):
            query = qkv[head, low:high, :]
            last = causal(dot_rt(query, qkv[heads + head, low:high, :]))
            scores.append((last, dot_rt(query, qkv[heads + head, 0:low, :]) if low else None))
        logs, outs = [], []
        for head, (last, first) in enumerate(scores):
            top = jnp.max(last, axis=1, keepdims=True)
            if low:
                top = jnp.maximum(top, jnp.max(first, axis=1, keepdims=True))
                first = jnp.exp(first - top)
            last = jnp.exp(last - top)
            total = jnp.sum(last, axis=1, keepdims=True)
            if low:
                total = total + jnp.sum(first, axis=1, keepdims=True)
            inverse = 1.0 / total
            out = dot((last * inverse).astype(bf16), qkv[2 * heads + head, low:high, :])
            if low:
                out = out + dot((first * inverse).astype(bf16), qkv[2 * heads + head, 0:low, :])
            outs.append(out)
            logs.append(top + jnp.log(total))
        wide_ref[low:high, :] = cat(outs, 1)
        log_ref[low:high, :] = cat(logs, 1)

    piece = length // 4
    x, c = place_ref[0], place_ref[2]
    for target, col in ((own_ref, x), (send_ref, 1 - x)):
        for i, core in enumerate((c, 1 - c)):
            start = pl.multiple_of((2 * core + col) * piece, piece)
            target[i * piece : (i + 1) * piece, :] = wide_ref[pl.ds(start, piece), :].astype(bf16)


def backward_kernel(
    heads, place_ref, qkv_ref, log_ref, wide_ref, keep_ref, got_ref, turned_ref, extra_ref,
    grad_ref, own_ref, send_ref, bias_ref,
    qkv, ups, dots, grads, key_sum, value_sum,
):
    length = qkv_ref.shape[0]
    split_heads(qkv_ref, qkv, 3 * heads, heads)
    piece = length // 4
    x, c = place_ref[0], place_ref[2]
    for source, col in ((keep_ref, x), (got_ref, 1 - x)):
        for i, core in enumerate((c, 1 - c)):
            start = pl.multiple_of((2 * core + col) * piece, piece)
            values = source[i * piece : (i + 1) * piece, :]
            wide = wide_ref[pl.ds(start, piece), :] * values.astype(f32)
            for j in range(heads):
                ups[j, pl.ds(start, piece), :] = values[:, j * HD : (j + 1) * HD]
                dots[j, pl.ds(start, piece), :] = jnp.sum(
                    wide[:, j * HD : (j + 1) * HD], axis=1, keepdims=True
                )

    key_sum[...] = jnp.zeros_like(key_sum)
    value_sum[...] = jnp.zeros_like(value_sum)
    for low in range(0, length, QB):
        high = low + QB
        sums = [0.0] * heads
        spans = [(low, high)] + ([(0, low)] if low else [])
        for start, stop in spans:
            first = []
            for head in range(heads):
                scores = dot_rt(qkv[head, low:high, :], qkv[heads + head, start:stop, :])
                if start == low:
                    scores = causal(scores)
                first.append((scores, dot_rt(ups[head, low:high, :], qkv[2 * heads + head, start:stop, :])))
            for head in range(heads):
                query = qkv[head, low:high, :]
                up = ups[head, low:high, :]
                key = qkv[heads + head, start:stop, :]
                scores, prob_grad = first[head]
                probs = jnp.exp(scores - log_ref[low:high, head : head + 1])
                score_grad = (probs * (prob_grad - dots[head, low:high, :])).astype(bf16)
                value_sum[head, :, start:stop] += dot_lt(up, probs.astype(bf16))
                key_sum[head, :, start:stop] += dot_lt(query, score_grad)
                sums[head] = sums[head] + dot(score_grad, key)
        for head in range(heads):
            grads[head, low:high, :] = (sums[head] * HD**-0.5).astype(bf16)
    for head in range(heads):
        grads[heads + head] = key_sum[head].T.astype(bf16)
        grads[2 * heads + head] = value_sum[head].T.astype(bf16)
    half = own_ref.shape[0]
    grad_ref[...] = cat([grads[i] for i in range(3 * heads)], 1)
    total = dot(turned_ref[...], grad_ref[...])
    own_ref[...] = total[:half]
    send_ref[:, : total.shape[1]] = total[half:].astype(bf16)
    end = total.shape[1] + extra_ref.shape[1]
    send_ref[:, total.shape[1] : end] = extra_ref[...]
    send_ref[:, end:] = jnp.zeros((half, send_ref.shape[1] - end), bf16)
    bias_ref[...] = jnp.sum(grad_ref[...].astype(f32), axis=0, keepdims=True)


def whole(shape):
    return pl.BlockSpec(shape, lambda head: (0,) * len(shape))


COST = pl.CostEstimate(flops=1, bytes_accessed=1, transcendentals=0)
LONG = pl.CostEstimate(flops=4 * 10**10, bytes_accessed=1, transcendentals=0)
SCALARS = pl.BlockSpec(memory_space=pltpu.SMEM)


def struct(dtype, *shape):
    return jax.ShapeDtypeStruct(shape, dtype)


def attend(place, first_all, keep, got, bias):
    length = first_all.shape[0]
    width = keep.shape[1]
    heads = width // (3 * HD)
    shapes = [
        struct(bf16, length, width),
        struct(bf16, length // 2, heads * HD),
        struct(bf16, length // 2, heads * HD),
        struct(f32, length, heads),
        struct(f32, length, heads * HD),
    ]
    return pl.pallas_call(
        functools.partial(forward_kernel, heads),
        name="attend",
        grid=(1,),
        in_specs=[SCALARS] + [whole(v.shape) for v in (first_all, keep, got, bias)],
        out_specs=[whole(v.shape) for v in shapes],
        out_shape=shapes,
        scratch_shapes=[
            pltpu.VMEM((first_all.shape[1], width), bf16),
            pltpu.VMEM((3 * heads, length, HD), bf16),
        ],
        compiler_params=pltpu.CompilerParams(vmem_limit_bytes=48 * 2**20),
        cost_estimate=LONG,
    )(place, first_all, keep, got, bias)


def attend_back(place, qkv, log, wide, keep, got, turned, extra):
    length, width = qkv.shape
    heads = width // (3 * HD)
    half = turned.shape[0] // 2
    shapes = [
        struct(bf16, length, width),
        struct(f32, half, width),
        struct(bf16, half, -(-(width + extra.shape[1]) // 128) * 128),
        struct(f32, 1, width),
    ]
    return pl.pallas_call(
        functools.partial(backward_kernel, heads),
        name="attend_back",
        grid=(1,),
        in_specs=[SCALARS] + [whole(v.shape) for v in (qkv, log, wide, keep, got, turned, extra)],
        out_specs=[whole(v.shape) for v in shapes],
        out_shape=shapes,
        scratch_shapes=[
            pltpu.VMEM((3 * heads, length, HD), bf16),
            pltpu.VMEM((heads, length, HD), bf16),
            pltpu.VMEM((heads, length, 1), f32),
            pltpu.VMEM((3 * heads, length, HD), bf16),
            pltpu.VMEM((heads, HD, length), f32),
            pltpu.VMEM((heads, HD, length), f32),
        ],
        compiler_params=pltpu.CompilerParams(vmem_limit_bytes=52 * 2**20),
        cost_estimate=LONG,
    )(place, qkv, log, wide, keep, got, turned, extra)


def layer_norm(values):
    center = jnp.mean(values, axis=1, keepdims=True)
    inverse = lax.rsqrt(jnp.mean(values * values, axis=1, keepdims=True) - center * center + EPS)
    return (values - center) * inverse, inverse


def norm_back(upstream, normed, inverse, gain):
    scaled = upstream * gain
    return inverse * (
        scaled
        - jnp.mean(scaled, axis=1, keepdims=True)
        - normed * jnp.mean(scaled * normed, axis=1, keepdims=True)
    )


def cat(parts, axis):
    return jnp.concatenate(parts, axis=axis)


VECTOR = pl.BlockSpec(memory_space=pltpu.VMEM)
ANYWHERE = pl.BlockSpec(memory_space=pl.ANY)


def call(kernel, name, place, inputs, shapes, scratch=(), spaces=None, cost=COST):
    ins, outs = spaces or ([VECTOR] * len(inputs), [VECTOR] * len(shapes))
    return pl.pallas_call(
        kernel,
        name=name,
        in_specs=[SCALARS] + list(ins),
        out_specs=list(outs),
        out_shape=list(shapes),
        scratch_shapes=list(scratch),
        compiler_params=pltpu.CompilerParams(vmem_limit_bytes=48 * 2**20),
        cost_estimate=cost,
    )(place, *inputs)


def first_norm_kernel(
    place_ref, own_ref, other_ref, core_own_ref, core_other_ref, params_ref,
    all_ref, turned_ref, chip_ref,
):
    x, c = place_ref[0], place_ref[2]
    span = own_ref.shape[0]
    piece = span // 2
    for i, (left, right) in enumerate(((own_ref, other_ref), (core_own_ref, core_other_ref))):
        start = pl.multiple_of((c if i == 0 else 1 - c) * span, span)
        values = cat((left[...], right[...]), 1).astype(f32)
        normed, _ = layer_norm(values)
        rounded = (normed * params_ref[0:1] + params_ref[1:2]).astype(bf16)
        all_ref[pl.ds(start, span), :] = rounded
        turned_ref[:, pl.ds(start, span)] = rounded.T
        rows = pl.ds(pl.multiple_of(x * piece, piece), piece)
        chip_ref[i * piece : (i + 1) * piece, :] = cat((left[rows, :], right[rows, :]), 1)


def upstream_kernel(place_ref, own_ref, side_ref, core_ref, all_ref, turned_ref):
    piece = own_ref.shape[0]
    pieces = ((own_ref, side_ref.at[piece:]), (core_ref.at[:piece], core_ref.at[piece:]))
    for i, (left, right) in enumerate(pieces):
        values = cat((left[...], right[...]), 1)
        all_ref[i * piece : (i + 1) * piece, :] = values
        turned_ref[:, i * piece : (i + 1) * piece] = values.T


def pack_qkv_kernel(place_ref, query_hbm, key_hbm, value_hbm, all_ref, parts, sems):
    copies = [
        pltpu.make_async_copy(source, parts.at[i], sems.at[i])
        for i, source in enumerate((query_hbm, key_hbm, value_hbm))
    ]
    for copy in copies:
        copy.start()
    for copy in copies:
        copy.wait()
    all_ref[...] = cat((parts[0], parts[1], parts[2]), 1)


def pack_kernel(
    place_ref, up_ref, down_ref, out_ref, cot_ref, first, second, keep_ref, send_ref, sum_ref
):
    x, lead = place_ref[0], place_ref[3]
    half = first.shape[1]
    piece = keep_ref.shape[0]
    for i, target in ((lead, first), (1 - lead, second)):
        units = pl.ds(pl.multiple_of(i * half, half), half)
        target[:half] = up_ref[:, units]
        target[half : 2 * half] = down_ref[units]
    second[2 * half :] = out_ref[...]
    for target, col in ((keep_ref, x), (send_ref, 1 - x)):
        target[...] = cot_ref[pl.ds(pl.multiple_of(col * piece, piece), piece), :]
    sum_ref[...] = jnp.sum(cot_ref[...].astype(f32), axis=0, keepdims=True)


def out_kernel(place_ref, keep_ref, got_ref, weight_ref, sum_ref, *send_refs):
    lined = place_ref[0] == place_ref[1]
    keep, got = keep_ref[...], got_ref[...]
    values = cat((jnp.where(lined, keep, got), jnp.where(lined, got, keep)), 1)
    total = dot(values, weight_ref[...])
    sum_ref[...] = total
    rows = send_refs[0].shape[0]
    for i, send_ref in enumerate(send_refs):
        send_ref[...] = total[i * rows : (i + 1) * rows].astype(bf16)


def unit_tiles(count):
    step = 768
    return [(low, min(low + step, count)) for low in range(0, count, step)]


def unit_kernel(
    place_ref, params_ref, bias_ref, sum_hbm, got0, got1, chip_hbm, upstream_hbm, turned_hbm,
    own0, own1, beside0, beside1, above0, above1, across0, across1,
    middle_hbm, back_hbm, back0, back1, own0_g, own1_g, beside_g, above_g, across0_g, across1_g,
    result_hbm, result_send_hbm, bias_sum_ref,
    sums, got, chip, upstream, turned, up, down, second, second_turned, hidden, grads,
    middle, back, back_send, own_g, pair_g, across_g, result, result_send, in_sems, out_sems,
):
    lead = place_ref[3]
    half = own0.shape[1]
    rows = piece = got0.shape[0]
    started, pending = [], []

    def fetch(source, target):
        copy = pltpu.make_async_copy(source, target, in_sems.at[len(started)])
        copy.start()
        started.append(copy)
        return copy

    def put(source, target):
        copy = pltpu.make_async_copy(source, target, out_sems.at[len(pending)])
        copy.start()
        pending.append(copy)

    first = [fetch(sum_hbm, sums), fetch(chip_hbm, chip)]
    for i, source in enumerate((got0, got1)):
        first.append(fetch(source, got.at[pl.ds((1 - i) * rows, rows)]))
    ups, downs = [], []
    for base, left, right in ((0, (own0, own1), (beside0, beside1)), (2, (above0, above1), (across0, across1))):
        for i in range(2):
            number = base + (lead if i == 0 else 1 - lead)
            units = pl.ds(pl.multiple_of(number * half, half), half)
            for j, source in enumerate((left[i], right[i])):
                features = pl.ds(j * half, half)
                ups.append(fetch(source.at[pl.ds(0, half)], up.at[features, units]))
                downs.append(fetch(source.at[pl.ds(half, half)], down.at[units, features]))
    downs.append(fetch(upstream_hbm, upstream))
    later = fetch(turned_hbm, turned)

    for copy in first:
        copy.wait()
    middle[...] = chip[...].astype(f32) + (sums[...] + got[...].astype(f32) + params_ref[4:5])
    put(middle, middle_hbm)
    normed, _ = layer_norm(middle[...])
    second[...] = (normed * params_ref[2:3] + params_ref[3:4]).astype(bf16)
    for copy in ups + downs:
        copy.wait()
    root = 0.7978845608028654
    total = None
    for low, high in unit_tiles(up.shape[1]):
        pre = dot(second[...], up[:, low:high]) + bias_ref[:, low:high]
        square = pre * pre
        curve = jnp.tanh(root * (pre + 0.044715 * (square * pre)))
        share = 0.5 * (1.0 + curve)
        hidden[:, low:high] = (pre * share).astype(bf16)
        slope = share + (0.5 * root) * pre * (1.0 - curve * curve) * (1.0 + 0.134145 * square)
        grad = (dot_rt(upstream[...], down[low:high, :]) * slope).astype(bf16)
        grads[:, low:high] = grad
        bias_sum_ref[:, low:high] = jnp.sum(grad.astype(f32), axis=0, keepdims=True)
        part = dot_rt(grad, up[:, low:high])
        total = part if total is None else total + part
    back[...] = total
    back_send[...] = total.astype(bf16)
    put(back, back_hbm)
    for i, target in enumerate((back0, back1)):
        put(back_send.at[pl.ds(i * rows, rows)], target)

    second_turned[...] = second[...].T
    later.wait()
    targets = (
        (own_g.at[0], own0_g, pair_g.at[0], beside_g.at[0]),
        (own_g.at[1], own1_g, pair_g.at[1], beside_g.at[1]),
        (pair_g.at[2], above_g.at[0], across_g.at[0], across0_g),
        (pair_g.at[3], above_g.at[1], across_g.at[1], across1_g),
    )
    for i in (3, 2, 1, 0):
        units = slice(i * half, (i + 1) * half)
        near, near_hbm, far, far_hbm = targets[i]
        for base, left, source in ((0, second_turned, grads), (half, turned, hidden)):
            total = dot(left[...], source[:, units])
            near[:, base : base + half] = total[:half].astype(near.dtype)
            far[:, base : base + half] = total[half:].astype(far.dtype)
        put(near, near_hbm)
        put(far, far_hbm)
    total = dot(hidden[...], down[...])
    result[...] = total[:piece]
    result_send[...] = total[piece:].astype(bf16)
    put(result, result_hbm)
    put(result_send, result_send_hbm)
    for copy in pending:
        copy.wait()


def unit_layer(place, params, bias, inputs, blocks):
    span, width = inputs[0].shape
    half = width // 2
    hid = blocks[0].shape[0]
    message, total = struct(bf16, half, hid), struct(f32, half, hid)
    shapes = (
        struct(f32, span, width), struct(f32, span, width),
        *[struct(bf16, span // 2, width)] * 2,
        total, total, struct(bf16, 2, half, hid), struct(bf16, 2, half, hid), message, message,
        struct(f32, half, width), struct(bf16, half, width), struct(f32, 1, 2 * hid),
    )
    scratch = (
        pltpu.VMEM((span, width), f32),
        pltpu.VMEM((span, width), bf16),
        pltpu.VMEM((span, width), bf16),
        pltpu.VMEM((span, width), bf16),
        pltpu.VMEM((width, span), bf16),
        pltpu.VMEM((width, 2 * hid), bf16),
        pltpu.VMEM((2 * hid, width), bf16),
        pltpu.VMEM((span, width), bf16),
        pltpu.VMEM((width, span), bf16),
        pltpu.VMEM((span, 2 * hid), bf16),
        pltpu.VMEM((span, 2 * hid), bf16),
        pltpu.VMEM((span, width), f32),
        pltpu.VMEM((span, width), f32),
        pltpu.VMEM((span, width), bf16),
        pltpu.VMEM((2, half, hid), f32),
        pltpu.VMEM((4, half, hid), bf16),
        pltpu.VMEM((2, half, hid), bf16),
        pltpu.VMEM((half, width), f32),
        pltpu.VMEM((half, width), bf16),
        pltpu.SemaphoreType.DMA((len(inputs) + 2 * len(blocks),)),
        pltpu.SemaphoreType.DMA((len(shapes) + 1,)),
    )
    return call(
        unit_kernel, "units", place, (params, bias, *inputs, *blocks), shapes, scratch,
        spaces=(
            [VECTOR] * 2 + [ANYWHERE] * (len(inputs) + len(blocks)),
            [ANYWHERE] * (len(shapes) - 1) + [VECTOR],
        ),
    )


def out_back_kernel(
    place_ref, back_ref, got0, got1, middle_ref, upstream_ref, params_ref, weight_ref,
    att_keep_ref, att_got_ref, own_ref, send_ref, grad_keep_ref, grad_send_ref, weight_own_ref, weight_send_ref, sums_ref,
    weight_sum,
):
    step = pl.program_id(0)
    lined = place_ref[0] == place_ref[1]
    half = own_ref.shape[1]
    part = att_keep_ref.shape[1]
    normed, inverse = layer_norm(middle_ref[...])
    rows = back_ref.shape[0]
    rows = pl.ds(pl.multiple_of(lax.rem(step, 2) * rows, rows), rows)
    got = jnp.where(step < 2, got1[rows, :], got0[rows, :])
    back = back_ref[...] + got.astype(f32)
    grad = upstream_ref[...].astype(f32) + norm_back(back, normed, inverse, params_ref[2:3])
    rounded = grad.astype(bf16)
    values = dot_rt(rounded, weight_ref[...]).astype(bf16)
    here, there = values[:, :part], values[:, part:]
    grad_keep_ref[...] = jnp.where(lined, here, there)
    grad_send_ref[...] = jnp.where(lined, there, here)
    keep, got = att_keep_ref[...], att_got_ref[...]
    att = cat((jnp.where(lined, keep, got), jnp.where(lined, got, keep)), 1)
    total = dot_lt(rounded, att)

    @pl.when(step == 0)
    def _():
        weight_sum[...] = total
        sums_ref[...] = jnp.zeros_like(sums_ref)

    @pl.when(step > 0)
    def _():
        weight_sum[...] += total

    @pl.when(step < pl.num_programs(0) // 2)
    def _():
        own_ref[...] = grad[:, :half]
        send_ref[...] = rounded[:, half:]
        sums_ref[0:1] += jnp.sum(back * normed, axis=0, keepdims=True)
        sums_ref[1:2] += jnp.sum(back, axis=0, keepdims=True)
        sums_ref[2:3] += jnp.sum(rounded.astype(f32), axis=0, keepdims=True)

    @pl.when(step == pl.num_programs(0) - 1)
    def _():
        weight_own_ref[...] = weight_sum[:half]
        weight_send_ref[...] = weight_sum[half:].astype(bf16)


def out_back(place, back, got, middle, upstream, params, weight, att_keep, att_got):
    span, width = back.shape
    half = width // 2
    part = att_keep.shape[1]
    steps = 4
    rows = span // steps
    tile = lambda n: pl.BlockSpec((rows, n), lambda i: (i, 0))
    first = lambda n: pl.BlockSpec((rows, n), lambda i: (jnp.minimum(i, steps // 2 - 1), 0))
    return pl.pallas_call(
        out_back_kernel,
        name="out_back",
        grid=(steps,),
        in_specs=[
            SCALARS, tile(width), *[whole(v.shape) for v in got], tile(width), tile(width), whole(params.shape),
            whole(weight.shape), tile(part), tile(part),
        ],
        out_specs=[
            first(half), first(half), tile(part), tile(part),
            whole((half, 2 * part)), whole((half, 2 * part)), whole((8, width)),
        ],
        out_shape=[
            struct(f32, span // 2, half),
            struct(bf16, span // 2, half),
            struct(bf16, span, part),
            struct(bf16, span, part),
            struct(f32, half, 2 * part),
            struct(bf16, half, 2 * part),
            struct(f32, 8, width),
        ],
        scratch_shapes=[pltpu.VMEM((width, 2 * part), f32)],
        compiler_params=pltpu.CompilerParams(vmem_limit_bytes=52 * 2**20),
        cost_estimate=COST,
    )(place, back, *got, middle, upstream, params, weight, att_keep, att_got)


def result_kernel(place_ref, own_ref, got_ref, middle_ref, params_ref, keep_ref, send_ref):
    piece, half = keep_ref.shape
    total = own_ref[...] + got_ref[...].astype(f32) + params_ref[5:6]
    result = (middle_ref[:piece] + total).astype(bf16)
    keep_ref[...] = result[:, :half]
    send_ref[...] = result[:, half:]


def first_back_kernel(place_ref, grad_ref, keep_ref, got_ref, own_ref, send0, send1):
    c = place_ref[2]
    span = own_ref.shape[0]
    piece = span // 2
    for target, start in (
        (send0, (1 - c) * span),
        (send1, (1 - c) * span + piece),
        (own_ref.at[:piece], c * span),
        (own_ref.at[piece:], c * span + piece),
    ):
        grads = grad_ref[pl.ds(pl.multiple_of(start, piece), piece), :]
        both = cat((dot_rt(grads, keep_ref[...]), dot_rt(grads, got_ref[...])), 1)
        target[...] = both.astype(target.dtype)


def pick_kernel(place_ref, own_ref, got_ref, out_ref, keep_ref, send_ref):
    lined = place_ref[0] == place_ref[1]
    width = own_ref.shape[1]
    part = width // 3
    own, got = own_ref[...], got_ref[:, :width].astype(f32)
    out = out_ref[...] + got_ref[:, width : width + 2 * part].astype(f32)
    keep_ref[...] = cat((jnp.where(lined, own, got), out[:, :part]), 1)
    send_ref[...] = cat((jnp.where(lined, got, own), out[:, part:]), 1).astype(bf16)


def row_sums(value):
    return cat((value, jnp.zeros((value.shape[0], 126), f32)), 1).T[:8]


def first_sum_kernel(
    place_ref, part_ref, got0, got1, left_ref, right_ref, params_ref,
    own_ref, send_ref, sums_ref, param_sums_ref,
):
    half = own_ref.shape[1]
    grad = part_ref[...] + cat((got0[...], got1[...]), 0).astype(f32)
    own_ref[...] = grad[:, :half]
    send_ref[...] = grad[:, half:].astype(bf16)
    normed, _ = layer_norm(cat((left_ref[...], right_ref[...]), 1).astype(f32))
    scaled = grad * params_ref[0:1]
    param_sums_ref[0:1] = jnp.sum(grad * normed, axis=0, keepdims=True)
    param_sums_ref[1:2] = jnp.sum(grad, axis=0, keepdims=True)
    sums_ref[...] = row_sums(
        cat(
            (
                jnp.sum(scaled, axis=1, keepdims=True),
                jnp.sum(scaled * normed, axis=1, keepdims=True),
            ),
            1,
        )
    )


def input_kernel(
    place_ref, own_ref, got_ref, sums_ref, sums_got_ref, left_ref, right_ref, params_ref,
    mid_keep_ref, mid_got_ref, grad_ref,
):
    x = place_ref[0]
    span, half = own_ref.shape
    piece = span // 2
    normed, inverse = layer_norm(cat((left_ref[...], right_ref[...]), 1).astype(f32))
    normed = normed[:, :half]
    grad = own_ref[...] + got_ref[...].astype(f32)
    got = [sums_got_ref[i : i + 1] for i in range(10, 14)]
    got = cat((cat(got[:2], 1), cat(got[2:], 1)), 0)
    sums = (sums_ref[0:2] + got) * (1.0 / (2 * half))
    sums = cat((sums, jnp.zeros((126, span), f32)), 0).T
    scaled = grad * params_ref[0:1, :half]
    grad_ref[...] = inverse * (scaled - sums[:, 0:1] - normed * sums[:, 1:2])
    rows = pl.ds(pl.multiple_of(x * piece, piece), piece)
    grad_ref[rows, :] += mid_keep_ref[...]
    rows = pl.ds(pl.multiple_of((1 - x) * piece, piece), piece)
    grad_ref[rows, :] += mid_got_ref[...].astype(f32)


def sum_dp(value):
    return lax.psum_scatter(value.astype(bf16), "dp", scatter_dimension=0, tiled=True).astype(f32)


def halve_dp(value, step):
    low = (lax.axis_index("dp") // step) % 2 == 0
    rows = value.shape[0] // 2
    keep = jnp.where(low, value[:rows], value[rows:])
    send = jnp.where(low, value[rows:], value[:rows]).astype(bf16)
    pairs = [(i, i ^ step) for i in range(lax.axis_size("dp"))]
    return keep + lax.ppermute(send, "dp", pairs).astype(f32)


def small_x_kernel(place_ref, unit_ref, qkv_ref, second_ref, first_ref, token_ref, send_ref):
    half = send_ref.shape[1]
    part = half // 2
    send_ref[...] = jnp.zeros_like(send_ref)
    for i in range(4):
        send_ref[i : i + 1] = unit_ref[:, i * half : (i + 1) * half]
    send_ref[4:5, :part] = qkv_ref[:, :part]
    send_ref[4:5, part:] = qkv_ref[:, 2 * part : 3 * part]
    send_ref[5:8] = second_ref[0:3, half:]
    send_ref[8:10] = first_ref[0:2, half:]
    for i in range(4):
        send_ref[10 + i : 11 + i] = token_ref[i // 2 : i // 2 + 1, i % 2 * half : (i % 2 + 1) * half]


def small_y_kernel(place_ref, own_ref, got_ref, second_ref, first_ref, cot_ref, keep_ref, send_ref):
    lined = place_ref[0] == place_ref[1]
    half = send_ref.shape[1]
    own, got = own_ref[...], got_ref[...]
    features = cat(
        (second_ref[0:3, :half] + got[5:8], first_ref[0:2, :half] + got[8:10], cot_ref[...]), 0
    )
    for target, units, bias in (
        (keep_ref, own[0:2] + got[0:2], jnp.where(lined, own[4:5], got[4:5])),
        (send_ref, own[2:4] + got[2:4], jnp.where(lined, got[4:5], own[4:5])),
    ):
        target[...] = jnp.zeros_like(target)
        target[0:2] = units
        target[2:3] = bias
        target[3:9] = features


def small_c_kernel(place_ref, own_ref, got_ref, sum_ref):
    sum_ref[...] = own_ref[...]
    sum_ref[3:9] += got_ref[3:9]


def local(
    tokens,
    query_weight,
    key_weight,
    value_weight,
    query_bias,
    value_bias,
    out_weight,
    out_bias,
    up_weight,
    up_bias,
    down_weight,
    down_bias,
    attn_gain,
    attn_shift,
    mlp_gain,
    mlp_shift,
    cotangent,
):
    x = lax.axis_index("col")
    row = lax.axis_index("row")
    y, c = row // 2, row % 2
    z = lax.axis_index("dp")
    n_dp = lax.axis_size("dp")
    lined = x == y
    where = jnp.stack((x, y, c, z % 2)).astype(jnp.int32)
    span, half = tokens.shape
    piece = span // 2
    width = 2 * half
    length = 2 * span
    part = query_weight.shape[1]
    hid = up_weight.shape[1]

    def pick(first, second):
        return jnp.where(lined, first, second), jnp.where(lined, second, first)

    other_tokens = swap_x(tokens)
    (qkv_own,) = call(
        pack_qkv_kernel,
        "pack_qkv",
        where,
        (query_weight, key_weight, value_weight),
        (struct(bf16, half, 3 * part),),
        scratch=(pltpu.VMEM((3, half, part), bf16), pltpu.SemaphoreType.DMA((3,))),
        spaces=([ANYWHERE] * 3, [VECTOR]),
    )
    qkv_other = swap_y(qkv_own)
    core_tokens = swap_c(tokens)
    core_other = swap_c(other_tokens)
    qkv_keep, qkv_send = pick(qkv_own, qkv_other)
    qkv_got = swap_x(qkv_send)
    params = jnp.stack((attn_gain, attn_shift, mlp_gain, mlp_shift, out_bias, down_bias))
    params = cat((params, jnp.zeros((2, half), f32)), 0)
    params = cat((params, swap_x(params)), 1)
    by_unit = cat((query_bias, value_bias, up_bias), 0)
    by_unit_other = swap_y(by_unit)
    unit_keep, _ = pick(by_unit, by_unit_other)
    qkv_bias = cat((unit_keep[:part], jnp.zeros((part,), f32), unit_keep[part : 2 * part]), 0)[None]
    up_bias_all = cat((by_unit[2 * part :], by_unit_other[2 * part :]), 0)[None]

    own0, own1, cot_keep, cot_send, cot_sum = call(
        pack_kernel,
        "pack",
        where,
        (up_weight, down_weight, out_weight, cotangent),
        (
            struct(bf16, hid, half), struct(bf16, hid + part, half),
            struct(bf16, piece, half), struct(bf16, piece, half), struct(f32, 1, half),
        ),
    )
    own0_y, own1_y, _ = lax.optimization_barrier((own0, own1, qkv_other))
    above0, above1 = swap_y(own0_y), swap_y(own1_y)
    out_pair = cat((out_weight, above1[2 * half :]), 0)

    first_all, first_turned, chip = call(
        first_norm_kernel,
        "first_norm",
        where,
        (tokens, other_tokens, core_tokens, core_other, params),
        (struct(bf16, length, width), struct(bf16, width, length), struct(bf16, span, width)),
    )
    own0_x, qkv_got, first_all = lax.optimization_barrier((own0, qkv_got, first_all))
    beside0 = swap_x(own0_x)
    side = cat((out_pair, cot_send), 0)
    qkv, att_keep, att_send, logsum, wide = attend(where, first_all, qkv_keep, qkv_got, qkv_bias)
    att_send, side, beside0, above1 = lax.optimization_barrier((att_send, side, beside0, above1))
    att_got, side, above0 = lax.optimization_barrier((swap_x(att_send), swap_x(side), above0))
    beside1 = swap_z(beside0)
    across0, across1 = swap_y(beside0), swap_x(above1[: 2 * half])
    blocks = (own0, own1, beside0, beside1, above0, above1, across0, across1)
    upstream, upstream_turned = call(
        upstream_kernel,
        "upstream",
        where,
        (cot_keep, side, swap_c(cat((cot_keep, side[half:]), 0))),
        (struct(bf16, span, width), struct(bf16, width, span)),
    )
    out_all = cat((out_pair, side[:half]), 1)
    out_sum, *out_send = call(
        out_kernel,
        "out_projection",
        where,
        (att_keep, att_got, out_all),
        (struct(f32, span, width), *[struct(bf16, span // 2, width)] * 2),
        cost=LONG,
    )
    out_got = [swap_c(v) for v in out_send]
    (
        middle, back, *back_send,
        own0_g, own1_g, beside_g, above_g, across0_g, across1_g,
        result_own, result_send, up_bias_sum,
    ) = unit_layer(
        where, params, up_bias_all, (out_sum, *out_got, chip, upstream, upstream_turned), blocks
    )
    back_got = [swap_c(v) for v in back_send]
    across0_got, across1_got = swap_y(across0_g), swap_x(across1_g)

    (
        mid_keep, mid_send, grad_keep, grad_send, out_own_g, out_send_g, second_sums,
    ) = out_back(where, back, back_got, middle, upstream, params, out_all, att_keep, att_got)
    grad_got = swap_x(grad_send)
    beside_g, above_g, across0_got, across1_got, grad_got = lax.optimization_barrier(
        (beside_g, above_g, across0_got, across1_got, grad_got)
    )
    add = lambda first, second: (first.astype(f32) + second.astype(f32)).astype(bf16)
    beside_got = swap_x(jnp.stack((add(beside_g[0], across0_got), beside_g[1])))
    above_got = swap_y(jnp.stack((above_g[0], add(above_g[1], across1_got))))
    qkv_grad, qkv_own_g, qkv_send_g, qkv_bias_sum = attend_back(
        where, qkv, logsum, wide, grad_keep, grad_got, first_turned, out_send_g
    )
    qkv_got_g = swap_x(qkv_send_g)

    part_own, *part_send = call(
        first_back_kernel,
        "first_back",
        where,
        (qkv_grad, qkv_keep, qkv_got),
        (struct(f32, span, width), *[struct(bf16, piece, width)] * 2),
    )
    first_own, first_send, first_sums, attn_sums = call(
        first_sum_kernel,
        "first_sum",
        where,
        (part_own, *[swap_c(v) for v in part_send], tokens, other_tokens, params),
        (
            struct(f32, span, half), struct(bf16, span, half), struct(f32, 8, span),
            struct(f32, 8, width),
        ),
    )
    first_got = swap_x(first_send)
    first_own, beside_got, above_got = lax.optimization_barrier((first_own, beside_got, above_got))
    others = beside_got.astype(f32) + above_got.astype(f32)
    late = cat((own0_g + others[0], own1_g + others[1]), 1).astype(bf16)
    row_shape = struct(f32, 16, half)
    (small_x,) = call(
        small_x_kernel,
        "small_x",
        where,
        (up_bias_sum, qkv_bias_sum, second_sums, attn_sums, first_sums),
        (row_shape,),
    )
    late, small_x = lax.optimization_barrier((late, small_x))
    mid_send, qkv_got_g, sums_got = lax.optimization_barrier((mid_send, qkv_got_g, swap_x(small_x)))
    late = sum_dp(late)
    att_keep_g, att_send_g = call(
        pick_kernel,
        "pick",
        where,
        (qkv_own_g, qkv_got_g, out_own_g),
        (struct(f32, half, 4 * part), struct(bf16, half, 4 * part)),
    )
    att_got_g = swap_y(att_send_g).astype(f32)
    small, send = call(
        small_y_kernel,
        "small_y",
        where,
        (small_x, sums_got, second_sums, attn_sums, cot_sum),
        (row_shape, row_shape),
    )
    att_got_g, small_got = lax.optimization_barrier((att_got_g, swap_y(send)))
    small = small + small_got
    (small,) = call(small_c_kernel, "small_c", where, (small, swap_c(small)), (row_shape,))
    first_got, result_own, small = lax.optimization_barrier((first_got, result_own, small))
    att_w_grad = att_keep_g + att_got_g
    steps = [n_dp >> i for i in range(1, n_dp.bit_length())]
    for i, step in enumerate(steps):
        att_w_grad = halve_dp(att_w_grad, step)
        if i == 0:
            att_w_grad, late, small = lax.optimization_barrier((att_w_grad, late, small))
    for step in steps:
        small = small + lax.ppermute(small, "dp", [(i, i ^ step) for i in range(n_dp)])
    qkv_w_grad = att_w_grad[:, : 3 * part]
    out_w_grad = att_w_grad[:, 3 * part :].T
    step = hid // 2
    up_w_grad = cat((late[:, :step], late[:, hid : hid + step]), 1)
    down_w_grad = cat((late[:, step:hid], late[:, hid + step :]), 1).T

    mid_got = swap_x(mid_send)
    (input_grad,) = call(
        input_kernel,
        "input_grad",
        where,
        (
            first_own, first_got, first_sums, sums_got, tokens, other_tokens,
            params, mid_keep, mid_got,
        ),
        (struct(f32, span, half),),
    )
    keep, send = call(
        result_kernel,
        "result",
        where,
        (result_own, swap_c(result_send), middle, params),
        (struct(bf16, piece, half), struct(bf16, piece, half)),
    )
    send, first_got = lax.optimization_barrier((send, first_got))
    got = swap_x(send)
    outputs = cat(
        (jnp.where(x == 0, keep, got), jnp.where(x == 0, got, keep)), 0
    )

    def take(value, size):
        chunk = size // n_dp
        return lax.dynamic_slice(value.reshape(-1), (z * chunk,), (chunk,))

    return (
        outputs,
        input_grad,
        qkv_w_grad[:, :part],
        qkv_w_grad[:, part : 2 * part],
        qkv_w_grad[:, 2 * part :],
        take(small[2, :part], part),
        take(small[2, part:], part),
        out_w_grad,
        take(small[5], half),
        up_w_grad,
        take(small[:2], hid),
        down_w_grad,
        take(small[8], half),
        take(small[6], half),
        take(small[7], half),
        take(small[3], half),
        take(small[4], half),
    )


def solution(mesh):
    placed = (
        P(("dp", "row"), "col"),
        P("col", "row"),
        P("col", "row"),
        P("col", "row"),
        P("row"),
        P("row"),
        P("row", "col"),
        P("col"),
        P("col", "row"),
        P("row"),
        P("row", "col"),
        P("col"),
        P("col"),
        P("col"),
        P("col"),
        P("col"),
        P(("dp", "row"), "col"),
    )
    return jax.shard_map(
        local,
        mesh=mesh,
        in_specs=placed,
        out_specs=(
            P(("dp", "row"), "col"),
            P(("dp", "row"), "col"),
            P(("col", "dp"), "row"),
            P(("col", "dp"), "row"),
            P(("col", "dp"), "row"),
            P(("row", "dp")),
            P(("row", "dp")),
            P("row", ("col", "dp")),
            P(("col", "dp")),
            P(("col", "dp"), "row"),
            P(("row", "dp")),
            P("row", ("col", "dp")),
            P(("col", "dp")),
            P(("col", "dp")),
            P(("col", "dp")),
            P(("col", "dp")),
            P(("col", "dp")),
        ),
        check_vma=False,
    )
```
